32 devices in a mesh: dp: 4 (over z), tensor: 4 (over y, core), pipe: 2 (over x).
Axes of the slice: x: 2, y: 2, z: 4, core: 2. Of those that a mesh axis runs over, the one named last changes fastest.
Arguments:
- normed: bfloat16 [2, 1792, 16384], P('pipe', 'dp', 'tensor'), may hold values from -0.875 to 0.875
- w_value: bfloat16 [2, 16384, 1024], P('pipe', 'tensor'), may hold values from -0.5 to 0.5
- grad_value: bfloat16 [2, 1792, 1024], P('pipe', 'dp'), may hold values from -114688 to 114688
- assistant_mask: int32 [4, 4, 8192], P('dp'), may hold values from 0 to 1, as said below
Outputs:
- value_weight_grad: float32 [2, 4, 4096, 1024], P('pipe', 'tensor', 'dp')
- passed_grad: bfloat16 [2, 1792, 16384], P('pipe', 'dp', 'tensor')
The draws below stay inside these ranges and needn't reach their ends.
Inputs may be any that keep to these rules, and one draw needn't show every extreme that they name: `assistant_mask`: assistant tokens come in runs of whole turns; every packed sequence holds at least one assistant token.
All inputs are finite; a program needn't handle non-finite values.
Results may differ from the reference program's by a relative error of at most 0.015.
Values may be sent and summed in bfloat16 or wider, within the bound.
A program may use at most 64 MiB of HBM per device.

```python
import jax
import jax.numpy as jnp
from jax import lax

D = 16384
HEAD = 128
KV_HEADS = 8
TOK = 448
LEN = 8192
MICRO = 4
TOKENS = 1792
ROWS_PAD = 4096
N_DP = 4
N_TENSOR = 4
N_PIPE = 2


def draw_assistant_mask(key, part):
    span = max(LEN // 128, 1)
    turns = LEN // span
    draws = jax.random.randint(key, (N_DP, MICRO, turns), 0, 1000)
    replica = jnp.arange(N_DP, dtype=jnp.int32)[:, None, None]
    limit = 200 + 400 * replica // max(N_DP - 1, 1)
    active = (draws < limit).astype(jnp.int32)
    active = active.at[:, :, turns - 1].set(1)
    return jnp.repeat(active, span, axis=2).astype(jnp.int32)


def spiked(drawn, key, source, target, parts, factor):
    owner, partner = [(jnp.arange(drawn.shape[position]) // (drawn.shape[position] // parts)).reshape([-1 if axis == position else 1 for axis in range(drawn.ndim)]) for position in (source, target)]
    chosen = jax.random.permutation(key, parts)[partner]
    strong = (owner == chosen) | (owner == (partner + parts // 2) % parts)
    return jnp.where(strong, factor * drawn, drawn)


def level_of(rng, dims, shards, low, high):
    def one(position, blocks):
        heights = jax.random.uniform(jax.random.fold_in(jax.random.fold_in(rng, 6), position), (blocks,), jnp.float32, low / len(shards), high / len(shards))
        return jnp.repeat(jnp.exp(heights), dims[position] // blocks).reshape((-1,) + (1,) * (len(dims) - position - 1))

    gain = one(*shards[0])
    for cut in shards[1:]:
        gain = gain * one(*cut)
    return gain


def bell_draw(rng, extent, spread, reach, pieces=(), kind=jnp.bfloat16):
    drawn = spread * jax.random.normal(rng, extent, jnp.float32)
    if pieces:
        drawn = drawn * level_of(rng, extent, pieces, -0.22, 0.18)
    return jnp.clip(drawn, -reach, reach).astype(kind)


def heavy_noise(stream_key, dims, scale, most, shards, heavy, kind=jnp.bfloat16):
    drawn = scale * jax.random.normal(stream_key, dims, jnp.float32)
    if shards:
        drawn = drawn * level_of(stream_key, dims, shards, -0.22, 0.18)
    return jnp.clip(spiked(drawn, jax.random.fold_in(stream_key, 3), *heavy), -most, most).astype(kind)


def setup_inputs(seed: int = 0) -> dict:
    streams_of = jax.random.split(jax.random.key(seed), 5)
    return {
        "normed": heavy_noise(streams_of[0], (N_PIPE, TOKENS, D), 0.1, 0.875, ((0, 2), (1, 4), (2, 4)), (1, 2, 4, 2.0)),
        "w_value": bell_draw(streams_of[1], (N_PIPE, D, KV_HEADS * HEAD), HEAD ** -0.5, 0.5, ((0, 2), (1, 4))),
        "grad_value": bell_draw(streams_of[2], (N_PIPE, TOKENS, KV_HEADS * HEAD), (N_DP * MICRO * LEN // 7), 114688.0, ((0, 2), (1, 4))),
        "assistant_mask": draw_assistant_mask(jax.random.fold_in(streams_of[4], 71), 0),
    }


def reference(normed, w_value, grad_value, assistant_mask):
    mask_sum = jnp.sum(assistant_mask, dtype=jnp.int32)
    divisor = mask_sum.astype(jnp.float32)
    block_rows = D // N_TENSOR
    weight_grads = []
    input_grads = []
    for section in range(N_PIPE):
        inputs = normed[section]
        weight = w_value[section]
        upstream = grad_value[section]
        input_blocks = inputs.reshape(N_DP, TOK, D)
        upstream_blocks = upstream.reshape(N_DP, TOK, KV_HEADS * HEAD)

        def accumulate(carry, pair):
            block_in, block_up = pair
            term = jnp.dot(block_in.T, block_up, preferred_element_type=jnp.float32).astype(jnp.bfloat16)
            term = lax.optimization_barrier(term)
            return carry + term.astype(jnp.float32), None

        weight_sum, _ = lax.scan(accumulate, jnp.zeros((D, KV_HEADS * HEAD), jnp.float32), (input_blocks, upstream_blocks))
        scaled = (weight_sum / divisor).reshape(N_TENSOR, block_rows, KV_HEADS * HEAD)
        weight_grads.append(jnp.pad(scaled, ((0, 0), (0, ROWS_PAD - block_rows), (0, 0))))
        input_sum = jnp.zeros((TOKENS, D), jnp.float32)
        for head in range(KV_HEADS):
            piece_up = upstream[:, head * HEAD:(head + 1) * HEAD]
            piece_w = weight[:, head * HEAD:(head + 1) * HEAD]
            part = jnp.dot(piece_up, piece_w.T, preferred_element_type=jnp.float32).astype(jnp.bfloat16)
            part = lax.optimization_barrier(part)
            input_sum = input_sum + part.astype(jnp.float32)
        input_grads.append((input_sum / divisor).astype(jnp.bfloat16))
    passed = input_grads[1:] + [jnp.zeros((TOKENS, D), jnp.bfloat16)]
    return jnp.stack(weight_grads), jnp.stack(passed)
```

```python
import functools

import jax
import jax.numpy as jnp
from jax import lax
from jax.experimental import pallas as pl
from jax.experimental.pallas import tpu as pltpu
from jax.sharding import PartitionSpec as P

HEAD = 128
KV_HEADS = 8
LANES = 128
PACK = 16
MESH = pl.DeviceIdType.MESH


def from_behind(block, axis, distance):
    devices = range(lax.axis_size(axis))
    route = [(i - distance, i) for i in devices if i - distance in devices]
    return lax.ppermute(block, axis, route)


def pieces_of(extent, unit, most):
    for count in range(most, 0, -1):
        if extent % (count * unit) == 0:
            return count
    return 1


def exchange(
    replicas, tensors, sections, x_cuts, w_cuts,
    normed, weight, grad, mask,
    total, passed, count,
    mine, arrived, grads, weights, sending, counts,
    load_sem, w_sem, n_send, n_recv, g_send, g_recv, f_send, f_recv, c_send, c_recv, x_send, x_recv,
):
    dp = lax.axis_index("dp")
    tensor = lax.axis_index("tensor")
    pipe = lax.axis_index("pipe")
    rows = grads.shape[1]
    share = rows // tensors
    owned = mine.shape[1]
    step = passed.shape[1] // x_cuts

    def peer(d):
        return lax.rem(dp + d, replicas)

    def mate(e):
        return lax.rem(tensor + e, tensors)

    def part(index):
        return pl.ds(pl.multiple_of(index * share, PACK), share)

    def columns(index):
        return pl.ds(pl.multiple_of(index * owned, LANES), owned)

    grad_load = pltpu.make_async_copy(grad.at[0], grads.at[0], load_sem.at[0])
    grad_load.start()
    w_loads = [
        pltpu.make_async_copy(
            weight.at[0, pl.ds(c * step, step)], weights.at[pl.ds(c * step, step)], w_sem.at[c]
        )
        for c in range(x_cuts)
    ]

    @pl.when(pipe > 0)
    def _():
        for load in w_loads:
            load.start()

    mine_load = pltpu.make_async_copy(normed.at[0, :, columns(dp)], mine, load_sem.at[1])
    mine_load.start()

    barrier = pltpu.get_barrier_semaphore()
    for d in range(1, replicas):
        pl.semaphore_signal(barrier, inc=1, device_id={"dp": peer(d)}, device_id_type=MESH)
    for e in range(1, tensors):
        pl.semaphore_signal(barrier, inc=1, device_id={"tensor": mate(e)}, device_id_type=MESH)

    pl.semaphore_signal(
        barrier, inc=1, device_id={"pipe": lax.rem(pipe + 1, sections)}, device_id_type=MESH
    )
    pl.semaphore_wait(barrier, replicas - 1 + tensors - 1 + 1)

    g_copies = [
        pltpu.make_async_remote_copy(
            src_ref=grad.at[0, part(tensor)],
            dst_ref=grads.at[d, part(tensor)],
            send_sem=g_send.at[d],
            recv_sem=g_recv.at[d],
            device_id={"dp": peer(d)},
            device_id_type=MESH,
        )
        for d in range(1, replicas)
    ]
    n_copies = [
        pltpu.make_async_remote_copy(
            src_ref=normed.at[0, :, columns(peer(d))],
            dst_ref=arrived.at[d - 1],
            send_sem=n_send.at[d],
            recv_sem=n_recv.at[d],
            device_id={"dp": peer(d)},
            device_id_type=MESH,
        )
        for d in range(1, replicas)
    ]
    for copy in g_copies:
        copy.start()
    for copy in n_copies:
        copy.start()

    grad_load.wait()

    def x_copy(c):
        cut = pl.ds(c * step, step)
        return pltpu.make_async_remote_copy(
            src_ref=sending.at[:, cut],
            dst_ref=passed.at[:, cut],
            send_sem=x_send.at[c],
            recv_sem=x_recv.at[c],
            device_id={"pipe": lax.rem(pipe + sections - 1, sections)},
            device_id_type=MESH,
        )

    @pl.when(pipe > 0)
    def _():
        for c in range(x_cuts):
            w_loads[c].wait()
            sending[:, c * step : (c + 1) * step] = lax.dot_general(
                grads[0],
                weights[c * step : (c + 1) * step, :],
                (((1,), (1,)), ((), ())),
                preferred_element_type=jnp.float32,
            ).astype(sending.dtype)
            x_copy(c).start()

    counts[0] = jnp.full(counts.shape[1:], jnp.sum(mask[...], dtype=jnp.int32), jnp.int32)
    c_copies = [
        pltpu.make_async_remote_copy(
            src_ref=counts.at[0],
            dst_ref=counts.at[d],
            send_sem=c_send.at[d],
            recv_sem=c_recv.at[d],
            device_id={"dp": peer(d)},
            device_id_type=MESH,
        )
        for d in range(1, replicas)
    ]
    for copy in c_copies:
        copy.start()

    def forward(d, e):
        return pltpu.make_async_remote_copy(
            src_ref=grads.at[d, part(tensor)],
            dst_ref=grads.at[d, part(tensor)],
            send_sem=f_send.at[d, e],
            recv_sem=f_recv.at[d, e],
            device_id={"tensor": mate(e)},
            device_id_type=MESH,
        )

    forwards = [[forward(d, e) for e in range(1, tensors)] for d in range(1, replicas)]
    for d in range(1, replicas):
        g_copies[d - 1].wait_recv()
        for copy in forwards[d - 1]:
            copy.start()

    tile = owned // w_cuts

    def add(d, block):
        for k in range(w_cuts):
            cut = slice(k * tile, (k + 1) * tile)
            product = lax.dot_general(
                block[:, cut], grads[d], (((0,), (0,)), ((), ())), preferred_element_type=jnp.float32
            )
            if d == 0:
                total[cut, :] = product
            else:
                total[cut, :] += product

    mine_load.wait()
    add(0, mine)
    for copy in c_copies:
        copy.wait()
    whole = counts[0]
    for d in range(1, replicas):
        whole = whole + counts[d]
    count[...] = whole.astype(jnp.float32)
    for d in range(1, replicas):
        for copy in forwards[d - 1]:
            copy.wait_recv()
        n_copies[d - 1].wait_recv()
        add(d, arrived.at[d - 1])

    @pl.when(pipe < sections - 1)
    def _():
        for c in range(x_cuts):
            x_copy(c).wait_recv()

    @pl.when(pipe > 0)
    def _():
        for c in range(x_cuts):
            x_copy(c).wait_send()

    for d in range(1, replicas):
        g_copies[d - 1].wait_send()
        n_copies[d - 1].wait_send()
        for copy in forwards[d - 1]:
            copy.wait_send()


def finish(sections, cuts, total, passed, count, grad_out, passed_out, grad_part, passed_part, g_sem, p_sem):
    pipe = lax.axis_index("pipe")
    divisor = count[0:1, 0:1]
    high = total.shape[0] // cuts
    wide = passed.shape[1] // cuts
    copies = []
    for c in range(cuts):
        tall = slice(c * high, (c + 1) * high)
        cut = slice(c * wide, (c + 1) * wide)
        grad_part[tall, :] = total[tall, :] / divisor
        copy = pltpu.make_async_copy(
            grad_part.at[pl.ds(c * high, high)], grad_out.at[0, 0, pl.ds(c * high, high)], g_sem.at[c]
        )
        copy.start()
        copies.append(copy)

        @pl.when(pipe < sections - 1)
        def _():
            passed_part[:, cut] = (passed[:, cut].astype(jnp.float32) / divisor).astype(passed_part.dtype)

        @pl.when(pipe == sections - 1)
        def _():
            passed_part[:, cut] = jnp.zeros((passed.shape[0], wide), passed_part.dtype)

        copy = pltpu.make_async_copy(
            passed_part.at[:, pl.ds(c * wide, wide)], passed_out.at[0, :, pl.ds(c * wide, wide)], p_sem.at[c]
        )
        copy.start()
        copies.append(copy)
    for copy in copies:
        copy.wait()


def in_kernels(replicas, tensors, sections, normed, w_value, grad_value, assistant_mask):
    _, rows, width = normed.shape
    heads = w_value.shape[2]
    owned = width // replicas
    x_cuts = pieces_of(width, LANES, 8)
    w_cuts = pieces_of(owned, LANES, 4)
    out_cuts = pieces_of(owned, LANES, 4)
    kind = normed.dtype
    vmem = pl.BlockSpec(memory_space=pltpu.VMEM)
    anywhere = pl.BlockSpec(memory_space=pl.ANY)
    dma = pltpu.SemaphoreType.DMA
    size = kind.itemsize
    held = size * (rows * owned * replicas + replicas * rows * heads + width * heads + rows * width)
    held += 4 * assistant_mask.size + 4 * owned * heads + size * rows * width
    total, passed, count = pl.pallas_call(
        functools.partial(exchange, replicas, tensors, sections, x_cuts, w_cuts),
        out_shape=(
            pltpu.VMEM((owned, heads), jnp.float32),
            pltpu.VMEM((rows, width), kind),
            pltpu.VMEM((8, LANES), jnp.float32),
        ),
        in_specs=[anywhere, anywhere, anywhere, vmem],
        out_specs=(vmem, vmem, vmem),
        scratch_shapes=[
            pltpu.VMEM((rows, owned), kind),
            pltpu.VMEM((replicas - 1, rows, owned), kind),
            pltpu.VMEM((replicas, rows, heads), kind),
            pltpu.VMEM((width, heads), kind),
            pltpu.VMEM((rows, width), kind),
            pltpu.VMEM((replicas, 8, LANES), jnp.int32),
            dma((2,)),
            dma((x_cuts,)),
            dma((replicas,)),
            dma((replicas,)),
            dma((replicas,)),
            dma((replicas,)),
            dma((replicas, tensors)),
            dma((replicas, tensors)),
            dma((replicas,)),
            dma((replicas,)),
            dma((x_cuts,)),
            dma((x_cuts,)),
        ],
        compiler_params=pltpu.CompilerParams(
            collective_id=0, has_side_effects=True, vmem_limit_bytes=held + (8 << 20)
        ),
        name="exchange",
    )(normed, w_value, grad_value, assistant_mask)
    return pl.pallas_call(
        functools.partial(finish, sections, out_cuts),
        out_shape=(
            jax.ShapeDtypeStruct((1, 1, owned, heads), jnp.float32),
            jax.ShapeDtypeStruct((1, rows, width), kind),
        ),
        in_specs=[vmem, vmem, vmem],
        out_specs=(anywhere, anywhere),
        scratch_shapes=[
            pltpu.VMEM((owned, heads), jnp.float32),
            pltpu.VMEM((rows, width), kind),
            dma((out_cuts,)),
            dma((out_cuts,)),
        ],
        compiler_params=pltpu.CompilerParams(
            vmem_limit_bytes=2 * (4 * owned * heads + size * rows * width) + (8 << 20)
        ),
        name="finish",
    )(total, passed, count)


def with_collectives(normed, w_value, grad_value, assistant_mask):
    local_count = jnp.sum(assistant_mask, dtype=jnp.int32)
    mask_total = lax.psum(local_count, "dp")
    divisor = mask_total.astype(jnp.float32)
    inputs = normed[0]
    weight = w_value[0]
    upstream = grad_value[0]
    local_width = inputs.shape[1]
    replicas = lax.axis_size("dp")
    padded_rows = (local_width + replicas - 1) // replicas * replicas
    padded = jnp.pad(inputs, ((0, 0), (0, padded_rows - local_width)))
    weight_sum = lax.psum_scatter(
        lax.dot_general(
            padded, upstream, (((0,), (0,)), ((), ())), preferred_element_type=jnp.float32
        ).astype(jnp.bfloat16),
        "dp",
        scatter_dimension=0,
        tiled=True,
    ).astype(jnp.float32)
    total = jnp.zeros((upstream.shape[0], local_width), jnp.float32)
    for head in range(KV_HEADS):
        piece_up = upstream[:, head * HEAD : (head + 1) * HEAD]
        piece_w = weight[:, head * HEAD : (head + 1) * HEAD]
        part = lax.dot_general(
            piece_up, piece_w, (((1,), (1,)), ((), ())), preferred_element_type=jnp.float32
        ).astype(jnp.bfloat16)
        total = total + part.astype(jnp.float32)
    weight_grad = weight_sum / divisor
    input_grad = (total / divisor).astype(jnp.bfloat16)
    passed = from_behind(input_grad, "pipe", -1)
    return (weight_grad[None, None], passed[None])


def solution(mesh):
    replicas, tensors, sections = mesh.shape["dp"], mesh.shape["tensor"], mesh.shape["pipe"]

    def local(normed, w_value, grad_value, assistant_mask):
        _, rows, width = normed.shape
        aligned = width % (replicas * LANES) == 0 and rows % (tensors * PACK) == 0
        if aligned and min(replicas, tensors, sections) > 1:
            return in_kernels(replicas, tensors, sections, normed, w_value, grad_value, assistant_mask)
        return with_collectives(normed, w_value, grad_value, assistant_mask)

    return jax.shard_map(
        local,
        mesh=mesh,
        in_specs=(
            P("pipe", "dp", "tensor"),
            P("pipe", "tensor", None),
            P("pipe", "dp", None),
            P("dp", None, None),
        ),
        out_specs=(P("pipe", "tensor", "dp", None), P("pipe", "dp", "tensor")),
        check_vma=False,
    )
```

```python
import functools

import jax
import jax.numpy as jnp
from jax import lax
from jax.experimental import pallas as pl
from jax.experimental.pallas import tpu as pltpu
from jax.sharding import PartitionSpec as P

HEAD = 128
KV_HEADS = 8
LANES = 128
PACK = 16
MESH = pl.DeviceIdType.MESH


def from_behind(block, axis, distance):
    devices = range(lax.axis_size(axis))
    route = [(i - distance, i) for i in devices if i - distance in devices]
    return lax.ppermute(block, axis, route)


def pieces_of(extent, unit, most):
    for count in range(most, 0, -1):
        if extent % (count * unit) == 0:
            return count
    return 1


def exchange(
    replicas, tensors, sections, x_cuts, n_cuts,
    normed, weight, grad, mask,
    total, passed,
    mine, arrived, grads, weights, sending, counts, masks,
    load_sem, w_sem, n_send, n_recv, g_send, g_recv, f_send, f_recv, c_send, c_recv, x_send, x_recv,
):
    dp = lax.axis_index("dp")
    tensor = lax.axis_index("tensor")
    pipe = lax.axis_index("pipe")
    rows = grads.shape[1]
    share = rows // tensors
    owned = mine.shape[1]
    tile = owned // n_cuts
    step = passed.shape[1] // x_cuts
    bits = [1 << b for b in reversed(range(replicas.bit_length() - 1))]
    offsets = range(replicas - 1, 0, -1)

    def peer(d):
        return dp + sum(b * (1 - 2 * lax.rem(dp // b, 2)) for b in bits if d & b)

    def mate(e):
        return lax.rem(tensor + e, tensors)

    def part(index):
        return pl.ds(pl.multiple_of(index * share, PACK), share)

    def columns(index, k):
        return pl.ds(pl.multiple_of(index * owned + k * tile, LANES), tile)

    barrier = pltpu.get_barrier_semaphore()
    for d in offsets:
        pl.semaphore_signal(barrier, inc=1, device_id={"dp": peer(d)}, device_id_type=MESH)
    for e in range(1, tensors):
        pl.semaphore_signal(barrier, inc=1, device_id={"tensor": mate(e)}, device_id_type=MESH)
    pl.semaphore_signal(
        barrier, inc=1, device_id={"pipe": lax.rem(pipe + 1, sections)}, device_id_type=MESH
    )

    grad_load = pltpu.make_async_copy(grad.at[0], grads.at[0], load_sem.at[0])
    grad_load.start()
    w_loads = [
        pltpu.make_async_copy(
            weight.at[0, pl.ds(c * step, step)], weights.at[pl.ds(c * step, step)], w_sem.at[c]
        )
        for c in range(x_cuts)
    ]

    @pl.when(pipe > 0)
    def _():
        for load in w_loads:
            load.start()

    mask_load = pltpu.make_async_copy(mask.at[0], masks, load_sem.at[1])
    mask_load.start()
    mine_load = pltpu.make_async_copy(
        normed.at[0, :, pl.ds(pl.multiple_of(dp * owned, LANES), owned)], mine, load_sem.at[2]
    )
    mine_load.start()

    pl.semaphore_wait(barrier, replicas - 1 + tensors - 1 + 1)

    def g_copy(source, slot, b):
        return pltpu.make_async_remote_copy(
            src_ref=source,
            dst_ref=grads.at[slot + b, part(tensor)],
            send_sem=g_send.at[slot + b],
            recv_sem=g_recv.at[slot + b],
            device_id={"dp": peer(b)},
            device_id_type=MESH,
        )

    def n_copy(d, k):
        return pltpu.make_async_remote_copy(
            src_ref=normed.at[0, :, columns(peer(d), k)],
            dst_ref=arrived.at[d - 1, k],
            send_sem=n_send.at[d, k],
            recv_sem=n_recv.at[d, k],
            device_id={"dp": peer(d)},
            device_id_type=MESH,
        )

    def x_copy(c):
        cut = pl.ds(c * step, step)
        return pltpu.make_async_remote_copy(
            src_ref=sending.at[:, cut],
            dst_ref=passed.at[:, cut],
            send_sem=x_send.at[c],
            recv_sem=x_recv.at[c],
            device_id={"pipe": lax.rem(pipe + sections - 1, sections)},
            device_id_type=MESH,
        )

    def forward(d, e):
        return pltpu.make_async_remote_copy(
            src_ref=grads.at[d, part(tensor)],
            dst_ref=grads.at[d, part(tensor)],
            send_sem=f_send.at[d, e],
            recv_sem=f_recv.at[d, e],
            device_id={"tensor": mate(e)},
            device_id_type=MESH,
        )

    own = grad.at[0, part(tensor)]
    g_copies = {b: g_copy(own, 0, b) for b in bits}
    for b in bits:
        g_copies[b].start()
    ahead = min(2, n_cuts)
    n_copies = {(d, k): n_copy(d, k) for d in offsets for k in range(n_cuts)}
    for k in range(ahead):
        for d in offsets:
            n_copies[d, k].start()

    grad_load.wait()

    @pl.when(pipe > 0)
    def _():
        for c in range(x_cuts):
            w_loads[c].wait()
            sending[:, c * step : (c + 1) * step] = lax.dot_general(
                grads[0],
                weights[c * step : (c + 1) * step, :],
                (((1,), (1,)), ((), ())),
                preferred_element_type=jnp.float32,
            ).astype(sending.dtype)
            x_copy(c).start()

    mask_load.wait()
    counts[0] = jnp.full(counts.shape[1:], jnp.sum(masks[...], dtype=jnp.int32), jnp.int32)
    c_copies = [
        pltpu.make_async_remote_copy(
            src_ref=counts.at[0],
            dst_ref=counts.at[d],
            send_sem=c_send.at[d],
            recv_sem=c_recv.at[d],
            device_id={"dp": peer(d)},
            device_id_type=MESH,
        )
        for d in offsets
    ]
    for copy in c_copies:
        copy.start()

    forwards = {(d, e): forward(d, e) for d in offsets for e in range(1, tensors)}
    held = [0]
    for i, b in enumerate(bits):
        for slot in held:
            g_copies[slot + b].wait_recv()
            for later in bits[i + 1 :]:
                g_copies[slot + b + later] = g_copy(grads.at[slot + b, part(tensor)], slot + b, later)
                g_copies[slot + b + later].start()
            for e in range(1, tensors):
                forwards[slot + b, e].start()
        held = held + [slot + b for slot in held]

    for copy in c_copies:
        copy.wait()
    whole = counts[0]
    for d in offsets:
        whole = whole + counts[d]
    divisor = whole.astype(jnp.float32)[0:1, 0:1]

    def times(block, d):
        return lax.dot_general(
            block, grads[d], (((0,), (0,)), ((), ())), preferred_element_type=jnp.float32
        )

    mine_load.wait()
    for k in range(n_cuts):
        cut = slice(k * tile, (k + 1) * tile)
        total[cut, :] = times(mine[:, cut], 0)
    for d in offsets:
        for e in range(1, tensors):
            forwards[d, e].wait_recv()
    for k in range(n_cuts):
        cut = slice(k * tile, (k + 1) * tile)
        if k + ahead < n_cuts:
            for d in offsets:
                n_copies[d, k].wait_send()
                n_copies[d, k + ahead].start()
        if k == n_cuts - 1:

            @pl.when(pipe < sections - 1)
            def _():
                for c in range(x_cuts):
                    x_copy(c).wait_recv()
                    wide = slice(c * step, (c + 1) * step)
                    passed[:, wide] = (passed[:, wide].astype(jnp.float32) / divisor).astype(passed.dtype)

            @pl.when(pipe == sections - 1)
            def _():
                passed[...] = jnp.zeros(passed.shape, passed.dtype)

            @pl.when(pipe > 0)
            def _():
                for c in range(x_cuts):
                    x_copy(c).wait_send()

        for d in reversed(offsets):
            n_copies[d, k].wait_recv()
            if d == offsets[0]:
                total[cut, :] = (total[cut, :] + times(arrived[d - 1, k], d)) / divisor
            else:
                total[cut, :] += times(arrived[d - 1, k], d)

    for k in range(max(n_cuts - ahead, 0), n_cuts):
        for d in offsets:
            n_copies[d, k].wait_send()
    for d in offsets:
        g_copies[d].wait_send()
        for e in range(1, tensors):
            forwards[d, e].wait_send()


def finish(cuts, total, passed, grad_out, passed_out, g_sem, p_sem):
    high = total.shape[0] // cuts
    wide = passed.shape[1] // cuts
    copies = []
    for c in range(cuts):
        tall, cut = pl.ds(c * high, high), pl.ds(c * wide, wide)
        copies.append(pltpu.make_async_copy(total.at[tall], grad_out.at[0, 0, tall], g_sem.at[c]))
        copies.append(pltpu.make_async_copy(passed.at[:, cut], passed_out.at[0, :, cut], p_sem.at[c]))
    for copy in copies:
        copy.start()
    for copy in copies:
        copy.wait()


def in_kernels(replicas, tensors, sections, normed, w_value, grad_value, assistant_mask):
    _, rows, width = normed.shape
    heads = w_value.shape[2]
    owned = width // replicas
    x_cuts = pieces_of(width, LANES, 8)
    n_cuts = pieces_of(owned, LANES, 4)
    kind = normed.dtype
    vmem = pl.BlockSpec(memory_space=pltpu.VMEM)
    anywhere = pl.BlockSpec(memory_space=pl.ANY)
    dma = pltpu.SemaphoreType.DMA
    size = kind.itemsize
    held = size * (rows * owned * replicas + replicas * rows * heads + width * heads + rows * width)
    held += 4 * assistant_mask.size
    arguments = [
        pltpu.with_memory_space_constraint(array, pltpu.HBM)
        for array in (normed, w_value, grad_value, assistant_mask)
    ]
    total, passed = pl.pallas_call(
        functools.partial(exchange, replicas, tensors, sections, x_cuts, n_cuts),
        out_shape=(
            pltpu.VMEM((owned, heads), jnp.float32),
            pltpu.VMEM((rows, width), kind),
        ),
        in_specs=[anywhere] * 4,
        out_specs=(vmem, vmem),
        scratch_shapes=[
            pltpu.VMEM((rows, owned), kind),
            pltpu.VMEM((replicas - 1, n_cuts, rows, owned // n_cuts), kind),
            pltpu.VMEM((replicas, rows, heads), kind),
            pltpu.VMEM((width, heads), kind),
            pltpu.VMEM((rows, width), kind),
            pltpu.VMEM((replicas, 8, LANES), jnp.int32),
            pltpu.VMEM(assistant_mask.shape[1:], jnp.int32),
            dma((3,)),
            dma((x_cuts,)),
            dma((replicas, n_cuts)),
            dma((replicas, n_cuts)),
            dma((replicas,)),
            dma((replicas,)),
            dma((replicas, tensors)),
            dma((replicas, tensors)),
            dma((replicas,)),
            dma((replicas,)),
            dma((x_cuts,)),
            dma((x_cuts,)),
        ],
        compiler_params=pltpu.CompilerParams(
            collective_id=0, has_side_effects=True, vmem_limit_bytes=held + (8 << 20)
        ),
        name="exchange",
    )(*arguments)
    out_cuts = pieces_of(owned, LANES, 4)
    return pl.pallas_call(
        functools.partial(finish, out_cuts),
        out_shape=(
            jax.ShapeDtypeStruct((1, 1, owned, heads), jnp.float32),
            jax.ShapeDtypeStruct((1, rows, width), kind),
        ),
        in_specs=[vmem, vmem],
        out_specs=(anywhere, anywhere),
        scratch_shapes=[dma((out_cuts,)), dma((out_cuts,))],
        name="finish",
    )(total, passed)


def with_collectives(normed, w_value, grad_value, assistant_mask):
    local_count = jnp.sum(assistant_mask, dtype=jnp.int32)
    mask_total = lax.psum(local_count, "dp")
    divisor = mask_total.astype(jnp.float32)
    inputs = normed[0]
    weight = w_value[0]
    upstream = grad_value[0]
    local_width = inputs.shape[1]
    replicas = lax.axis_size("dp")
    padded_rows = (local_width + replicas - 1) // replicas * replicas
    padded = jnp.pad(inputs, ((0, 0), (0, padded_rows - local_width)))
    weight_sum = lax.psum_scatter(
        lax.dot_general(
            padded, upstream, (((0,), (0,)), ((), ())), preferred_element_type=jnp.float32
        ).astype(jnp.bfloat16),
        "dp",
        scatter_dimension=0,
        tiled=True,
    ).astype(jnp.float32)
    total = jnp.zeros((upstream.shape[0], local_width), jnp.float32)
    for head in range(KV_HEADS):
        piece_up = upstream[:, head * HEAD : (head + 1) * HEAD]
        piece_w = weight[:, head * HEAD : (head + 1) * HEAD]
        part = lax.dot_general(
            piece_up, piece_w, (((1,), (1,)), ((), ())), preferred_element_type=jnp.float32
        ).astype(jnp.bfloat16)
        total = total + part.astype(jnp.float32)
    weight_grad = weight_sum / divisor
    input_grad = (total / divisor).astype(jnp.bfloat16)
    passed = from_behind(input_grad, "pipe", -1)
    return (weight_grad[None, None], passed[None])


def solution(mesh):
    replicas, tensors, sections = mesh.shape["dp"], mesh.shape["tensor"], mesh.shape["pipe"]

    def local(normed, w_value, grad_value, assistant_mask):
        _, rows, width = normed.shape
        aligned = width % (replicas * LANES) == 0 and rows % (tensors * PACK) == 0
        aligned = aligned and replicas & (replicas - 1) == 0
        if aligned and min(replicas, tensors, sections) > 1:
            return in_kernels(replicas, tensors, sections, normed, w_value, grad_value, assistant_mask)
        return with_collectives(normed, w_value, grad_value, assistant_mask)

    return jax.shard_map(
        local,
        mesh=mesh,
        in_specs=(
            P("pipe", "dp", "tensor"),
            P("pipe", "tensor", None),
            P("pipe", "dp", None),
            P("dp", None, None),
        ),
        out_specs=(P("pipe", "tensor", "dp", None), P("pipe", "dp", "tensor")),
        check_vma=False,
    )
```

```python
import functools

import jax
import jax.numpy as jnp
from jax import lax
from jax.experimental import pallas as pl
from jax.experimental.pallas import tpu as pltpu
from jax.sharding import PartitionSpec as P

HEAD = 128
KV_HEADS = 8
LANES = 128
PACK = 16
MESH = pl.DeviceIdType.MESH


def from_behind(block, axis, distance):
    devices = range(lax.axis_size(axis))
    route = [(i - distance, i) for i in devices if i - distance in devices]
    return lax.ppermute(block, axis, route)


def pieces_of(extent, unit, most):
    for count in range(most, 0, -1):
        if extent % (count * unit) == 0:
            return count
    return 1


def exchange(
    replicas, tensors, sections, x_cuts, n_cuts,
    normed, weight, grad, mask,
    total, passed,
    mine, arrived, grads, weights, sending, counts, masks,
    load_sem, w_sem, n_send, n_recv, g_send, g_recv, f_send, f_recv, c_send, c_recv, x_send, x_recv,
):
    dp = lax.axis_index("dp")
    tensor = lax.axis_index("tensor")
    pipe = lax.axis_index("pipe")
    rows = grads.shape[1]
    share = rows // tensors
    owned = mine.shape[1]
    tile = owned // n_cuts
    step = passed.shape[1] // x_cuts
    bits = [1 << b for b in reversed(range(replicas.bit_length() - 1))]
    offsets = range(replicas - 1, 0, -1)

    def peer(d):
        return dp + sum(b * (1 - 2 * lax.rem(dp // b, 2)) for b in bits if d & b)

    def mate(e):
        return lax.rem(tensor + e, tensors)

    def part(index):
        return pl.ds(pl.multiple_of(index * share, PACK), share)

    def columns(index, k):
        return pl.ds(pl.multiple_of(index * owned + k * tile, LANES), tile)

    barrier = pltpu.get_barrier_semaphore()
    for d in offsets:
        pl.semaphore_signal(barrier, inc=1, device_id={"dp": peer(d)}, device_id_type=MESH)
    for e in range(1, tensors):
        pl.semaphore_signal(barrier, inc=1, device_id={"tensor": mate(e)}, device_id_type=MESH)
    pl.semaphore_signal(
        barrier, inc=1, device_id={"pipe": lax.rem(pipe + 1, sections)}, device_id_type=MESH
    )

    grad_load = pltpu.make_async_copy(grad.at[0], grads.at[0], load_sem.at[0])
    grad_load.start()
    w_loads = [
        pltpu.make_async_copy(
            weight.at[0, pl.ds(c * step, step)], weights.at[pl.ds(c * step, step)], w_sem.at[c]
        )
        for c in range(x_cuts)
    ]

    @pl.when(pipe > 0)
    def _():
        for load in w_loads:
            load.start()

    mask_load = pltpu.make_async_copy(mask.at[0], masks, load_sem.at[1])
    mask_load.start()
    mine_load = pltpu.make_async_copy(
        normed.at[0, :, pl.ds(pl.multiple_of(dp * owned, LANES), owned)], mine, load_sem.at[2]
    )
    mine_load.start()

    pl.semaphore_wait(barrier, replicas - 1 + tensors - 1 + 1)

    def g_copy(source, slot, b):
        return pltpu.make_async_remote_copy(
            src_ref=source,
            dst_ref=grads.at[slot + b, part(tensor)],
            send_sem=g_send.at[slot + b],
            recv_sem=g_recv.at[slot + b],
            device_id={"dp": peer(b)},
            device_id_type=MESH,
        )

    def n_copy(d, k):
        return pltpu.make_async_remote_copy(
            src_ref=normed.at[0, :, columns(peer(d), k)],
            dst_ref=arrived.at[d - 1, k],
            send_sem=n_send.at[d, k],
            recv_sem=n_recv.at[d, k],
            device_id={"dp": peer(d)},
            device_id_type=MESH,
        )

    def x_copy(c):
        cut = pl.ds(c * step, step)
        return pltpu.make_async_remote_copy(
            src_ref=sending.at[:, cut],
            dst_ref=passed.at[:, cut],
            send_sem=x_send.at[c],
            recv_sem=x_recv.at[c],
            device_id={"pipe": lax.rem(pipe + sections - 1, sections)},
            device_id_type=MESH,
        )

    def forward(d, e):
        return pltpu.make_async_remote_copy(
            src_ref=grads.at[d, part(tensor)],
            dst_ref=grads.at[d, part(tensor)],
            send_sem=f_send.at[d, e],
            recv_sem=f_recv.at[d, e],
            device_id={"tensor": mate(e)},
            device_id_type=MESH,
        )

    own = grad.at[0, part(tensor)]
    g_copies = {b: g_copy(own, 0, b) for b in bits}
    for b in bits:
        g_copies[b].start()
    ahead = min(2, n_cuts)
    n_copies = {(d, k): n_copy(d, k) for d in offsets for k in range(n_cuts)}
    for k in range(ahead):
        for d in offsets:
            n_copies[d, k].start()

    grad_load.wait()

    @pl.when(pipe > 0)
    def _():
        for c in range(x_cuts):
            w_loads[c].wait()
            sending[:, c * step : (c + 1) * step] = lax.dot_general(
                grads[0],
                weights[c * step : (c + 1) * step, :],
                (((1,), (1,)), ((), ())),
                preferred_element_type=jnp.float32,
            ).astype(sending.dtype)
            x_copy(c).start()

    mask_load.wait()
    counts[0] = jnp.full(counts.shape[1:], jnp.sum(masks[...], dtype=jnp.int32), jnp.int32)
    c_copies = [
        pltpu.make_async_remote_copy(
            src_ref=counts.at[0],
            dst_ref=counts.at[d],
            send_sem=c_send.at[d],
            recv_sem=c_recv.at[d],
            device_id={"dp": peer(d)},
            device_id_type=MESH,
        )
        for d in offsets
    ]
    for copy in c_copies:
        copy.start()

    forwards = {(d, e): forward(d, e) for d in offsets for e in range(1, tensors)}
    held = [0]
    for i, b in enumerate(bits):
        for slot in held:
            g_copies[slot + b].wait_recv()
            for later in bits[i + 1 :]:
                g_copies[slot + b + later] = g_copy(grads.at[slot + b, part(tensor)], slot + b, later)
                g_copies[slot + b + later].start()
            for e in range(1, tensors):
                forwards[slot + b, e].start()
        held = held + [slot + b for slot in held]

    for copy in c_copies:
        copy.wait()
    whole = counts[0]
    for d in offsets:
        whole = whole + counts[d]
    divisor = whole.astype(jnp.float32)[0:1, 0:1]

    def times(block, d):
        return lax.dot_general(
            block, grads[d], (((0,), (0,)), ((), ())), preferred_element_type=jnp.float32
        )

    mine_load.wait()
    for k in range(n_cuts):
        cut = slice(k * tile, (k + 1) * tile)
        total[cut, :] = times(mine[:, cut], 0)
    for k in range(n_cuts - ahead):
        for d in offsets:
            n_copies[d, k].wait_send()
            n_copies[d, k + ahead].start()
    for d in offsets:
        for e in range(1, tensors):
            forwards[d, e].wait_recv()
    for k in range(n_cuts):
        cut = slice(k * tile, (k + 1) * tile)
        if k == n_cuts - 1:

            @pl.when(pipe < sections - 1)
            def _():
                for c in range(x_cuts):
                    x_copy(c).wait_recv()
                    wide = slice(c * step, (c + 1) * step)
                    passed[:, wide] = (passed[:, wide].astype(jnp.float32) / divisor).astype(passed.dtype)

            @pl.when(pipe == sections - 1)
            def _():
                passed[...] = jnp.zeros(passed.shape, passed.dtype)

            @pl.when(pipe > 0)
            def _():
                for c in range(x_cuts):
                    x_copy(c).wait_send()

        for d in reversed(offsets):
            n_copies[d, k].wait_recv()
            if d == offsets[0]:
                total[cut, :] = (total[cut, :] + times(arrived[d - 1, k], d)) / divisor
            else:
                total[cut, :] += times(arrived[d - 1, k], d)

    for k in range(max(n_cuts - ahead, 0), n_cuts):
        for d in offsets:
            n_copies[d, k].wait_send()
    for d in offsets:
        g_copies[d].wait_send()
        for e in range(1, tensors):
            forwards[d, e].wait_send()


def finish(cuts, total, passed, grad_out, passed_out, g_sem, p_sem):
    high = total.shape[0] // cuts
    wide = passed.shape[1] // cuts
    copies = []
    for c in range(cuts):
        tall, cut = pl.ds(c * high, high), pl.ds(c * wide, wide)
        copies.append(pltpu.make_async_copy(total.at[tall], grad_out.at[0, 0, tall], g_sem.at[c]))
        copies.append(pltpu.make_async_copy(passed.at[:, cut], passed_out.at[0, :, cut], p_sem.at[c]))
    for copy in copies:
        copy.start()
    for copy in copies:
        copy.wait()


def in_kernels(replicas, tensors, sections, normed, w_value, grad_value, assistant_mask):
    _, rows, width = normed.shape
    heads = w_value.shape[2]
    owned = width // replicas
    x_cuts = pieces_of(width, LANES, 8)
    n_cuts = pieces_of(owned, LANES, 4)
    kind = normed.dtype
    vmem = pl.BlockSpec(memory_space=pltpu.VMEM)
    anywhere = pl.BlockSpec(memory_space=pl.ANY)
    dma = pltpu.SemaphoreType.DMA
    size = kind.itemsize
    held = size * (rows * owned * replicas + replicas * rows * heads + width * heads + rows * width)
    held += 4 * assistant_mask.size
    arguments = [
        pltpu.with_memory_space_constraint(array, pltpu.HBM)
        for array in (normed, w_value, grad_value, assistant_mask)
    ]
    total, passed = pl.pallas_call(
        functools.partial(exchange, replicas, tensors, sections, x_cuts, n_cuts),
        out_shape=(
            pltpu.VMEM((owned, heads), jnp.float32),
            pltpu.VMEM((rows, width), kind),
        ),
        in_specs=[anywhere] * 4,
        out_specs=(vmem, vmem),
        scratch_shapes=[
            pltpu.VMEM((rows, owned), kind),
            pltpu.VMEM((replicas - 1, n_cuts, rows, owned // n_cuts), kind),
            pltpu.VMEM((replicas, rows, heads), kind),
            pltpu.VMEM((width, heads), kind),
            pltpu.VMEM((rows, width), kind),
            pltpu.VMEM((replicas, 8, LANES), jnp.int32),
            pltpu.VMEM(assistant_mask.shape[1:], jnp.int32),
            dma((3,)),
            dma((x_cuts,)),
            dma((replicas, n_cuts)),
            dma((replicas, n_cuts)),
            dma((replicas,)),
            dma((replicas,)),
            dma((replicas, tensors)),
            dma((replicas, tensors)),
            dma((replicas,)),
            dma((replicas,)),
            dma((x_cuts,)),
            dma((x_cuts,)),
        ],
        compiler_params=pltpu.CompilerParams(
            collective_id=0, has_side_effects=True, vmem_limit_bytes=held + (8 << 20)
        ),
        name="exchange",
    )(*arguments)
    out_cuts = pieces_of(owned, LANES, 4)
    return pl.pallas_call(
        functools.partial(finish, out_cuts),
        out_shape=(
            jax.ShapeDtypeStruct((1, 1, owned, heads), jnp.float32),
            jax.ShapeDtypeStruct((1, rows, width), kind),
        ),
        in_specs=[vmem, vmem],
        out_specs=(anywhere, anywhere),
        scratch_shapes=[dma((out_cuts,)), dma((out_cuts,))],
        compiler_params=pltpu.CompilerParams(vmem_limit_bytes=8 << 20),
        name="finish",
    )(total, passed)


def with_collectives(normed, w_value, grad_value, assistant_mask):
    local_count = jnp.sum(assistant_mask, dtype=jnp.int32)
    mask_total = lax.psum(local_count, "dp")
    divisor = mask_total.astype(jnp.float32)
    inputs = normed[0]
    weight = w_value[0]
    upstream = grad_value[0]
    local_width = inputs.shape[1]
    replicas = lax.axis_size("dp")
    padded_rows = (local_width + replicas - 1) // replicas * replicas
    padded = jnp.pad(inputs, ((0, 0), (0, padded_rows - local_width)))
    weight_sum = lax.psum_scatter(
        lax.dot_general(
            padded, upstream, (((0,), (0,)), ((), ())), preferred_element_type=jnp.float32
        ).astype(jnp.bfloat16),
        "dp",
        scatter_dimension=0,
        tiled=True,
    ).astype(jnp.float32)
    total = jnp.zeros((upstream.shape[0], local_width), jnp.float32)
    for head in range(KV_HEADS):
        piece_up = upstream[:, head * HEAD : (head + 1) * HEAD]
        piece_w = weight[:, head * HEAD : (head + 1) * HEAD]
        part = lax.dot_general(
            piece_up, piece_w, (((1,), (1,)), ((), ())), preferred_element_type=jnp.float32
        ).astype(jnp.bfloat16)
        total = total + part.astype(jnp.float32)
    weight_grad = weight_sum / divisor
    input_grad = (total / divisor).astype(jnp.bfloat16)
    passed = from_behind(input_grad, "pipe", -1)
    return (weight_grad[None, None], passed[None])


def solution(mesh):
    replicas, tensors, sections = mesh.shape["dp"], mesh.shape["tensor"], mesh.shape["pipe"]

    def local(normed, w_value, grad_value, assistant_mask):
        _, rows, width = normed.shape
        aligned = width % (replicas * LANES) == 0 and rows % (tensors * PACK) == 0
        aligned = aligned and replicas & (replicas - 1) == 0
        if aligned and min(replicas, tensors, sections) > 1:
            return in_kernels(replicas, tensors, sections, normed, w_value, grad_value, assistant_mask)
        return with_collectives(normed, w_value, grad_value, assistant_mask)

    return jax.shard_map(
        local,
        mesh=mesh,
        in_specs=(
            P("pipe", "dp", "tensor"),
            P("pipe", "tensor", None),
            P("pipe", "dp", None),
            P("dp", None, None),
        ),
        out_specs=(P("pipe", "tensor", "dp", None), P("pipe", "dp", "tensor")),
        check_vma=False,
    )
```

```python
import functools

import jax
import jax.numpy as jnp
from jax import lax
from jax.experimental import pallas as pl
from jax.experimental.pallas import tpu as pltpu
from jax.sharding import PartitionSpec as P

HEAD = 128
KV_HEADS = 8
LANES = 128
PACK = 16
MESH = pl.DeviceIdType.MESH


def from_behind(block, axis, distance):
    devices = range(lax.axis_size(axis))
    route = [(i - distance, i) for i in devices if i - distance in devices]
    return lax.ppermute(block, axis, route)


def pieces_of(extent, unit, most):
    for count in range(most, 0, -1):
        if extent % (count * unit) == 0:
            return count
    return 1


def exchange(
    replicas, tensors, sections, x_cuts, n_cuts,
    normed, weight, grad, mask,
    total, passed, grads, last, scale,
    mine, arrived, weights, sending, counts, masks,
    load_sem, w_sem, n_send, n_recv, g_send, g_recv, f_send, f_recv, c_send, c_recv, x_send, x_recv,
):
    dp = lax.axis_index("dp")
    tensor = lax.axis_index("tensor")
    pipe = lax.axis_index("pipe")
    rows = grads.shape[1]
    share = rows // tensors
    owned = mine.shape[1]
    tile = owned // n_cuts
    step = passed.shape[1] // x_cuts
    bits = [1 << b for b in reversed(range(replicas.bit_length() - 1))]
    offsets = range(replicas - 1, 0, -1)

    def peer(d):
        return dp + sum(b * (1 - 2 * lax.rem(dp // b, 2)) for b in bits if d & b)

    def mate(e):
        return lax.rem(tensor + e, tensors)

    def part(index):
        return pl.ds(pl.multiple_of(index * share, PACK), share)

    def columns(index, k):
        return pl.ds(pl.multiple_of(index * owned + k * tile, LANES), tile)

    barrier = pltpu.get_barrier_semaphore()
    for d in offsets:
        pl.semaphore_signal(barrier, inc=1, device_id={"dp": peer(d)}, device_id_type=MESH)
    for e in range(1, tensors):
        pl.semaphore_signal(barrier, inc=1, device_id={"tensor": mate(e)}, device_id_type=MESH)
    pl.semaphore_signal(
        barrier, inc=1, device_id={"pipe": lax.rem(pipe + 1, sections)}, device_id_type=MESH
    )

    grad_load = pltpu.make_async_copy(grad.at[0], grads.at[0], load_sem.at[0])
    grad_load.start()
    w_loads = [
        pltpu.make_async_copy(
            weight.at[0, pl.ds(c * step, step)], weights.at[pl.ds(c * step, step)], w_sem.at[c]
        )
        for c in range(x_cuts)
    ]

    @pl.when(pipe > 0)
    def _():
        for load in w_loads:
            load.start()

    mask_load = pltpu.make_async_copy(mask.at[0], masks, load_sem.at[1])
    mask_load.start()
    mine_load = pltpu.make_async_copy(
        normed.at[0, :, pl.ds(pl.multiple_of(dp * owned, LANES), owned)], mine, load_sem.at[2]
    )
    mine_load.start()

    pl.semaphore_wait(barrier, replicas - 1 + tensors - 1 + 1)

    def g_copy(source, slot, b):
        return pltpu.make_async_remote_copy(
            src_ref=source,
            dst_ref=grads.at[slot + b, part(tensor)],
            send_sem=g_send.at[slot + b],
            recv_sem=g_recv.at[slot + b],
            device_id={"dp": peer(b)},
            device_id_type=MESH,
        )

    def n_copy(d, k):
        return pltpu.make_async_remote_copy(
            src_ref=normed.at[0, :, columns(peer(d), k)],
            dst_ref=last.at[d - 1] if k == n_cuts - 1 else arrived.at[d - 1, k],
            send_sem=n_send.at[d, k],
            recv_sem=n_recv.at[d, k],
            device_id={"dp": peer(d)},
            device_id_type=MESH,
        )

    def x_copy(c):
        cut = pl.ds(c * step, step)
        return pltpu.make_async_remote_copy(
            src_ref=sending.at[:, cut],
            dst_ref=passed.at[:, cut],
            send_sem=x_send.at[c],
            recv_sem=x_recv.at[c],
            device_id={"pipe": lax.rem(pipe + sections - 1, sections)},
            device_id_type=MESH,
        )

    def forward(d, e):
        return pltpu.make_async_remote_copy(
            src_ref=grads.at[d, part(tensor)],
            dst_ref=grads.at[d, part(tensor)],
            send_sem=f_send.at[d, e],
            recv_sem=f_recv.at[d, e],
            device_id={"tensor": mate(e)},
            device_id_type=MESH,
        )

    own = grad.at[0, part(tensor)]
    g_copies = {b: g_copy(own, 0, b) for b in bits}
    for b in bits:
        g_copies[b].start()
    ahead = min(2, n_cuts)
    n_copies = {(d, k): n_copy(d, k) for d in offsets for k in range(n_cuts)}
    for k in range(ahead):
        for d in offsets:
            n_copies[d, k].start()

    grad_load.wait()

    @pl.when(pipe > 0)
    def _():
        for c in range(x_cuts):
            w_loads[c].wait()
            sending[:, c * step : (c + 1) * step] = lax.dot_general(
                grads[0],
                weights[c * step : (c + 1) * step, :],
                (((1,), (1,)), ((), ())),
                preferred_element_type=jnp.float32,
            ).astype(sending.dtype)
            x_copy(c).start()

    mask_load.wait()
    counts[0] = jnp.full(counts.shape[1:], jnp.sum(masks[...], dtype=jnp.int32), jnp.int32)
    c_copies = [
        pltpu.make_async_remote_copy(
            src_ref=counts.at[0],
            dst_ref=counts.at[d],
            send_sem=c_send.at[d],
            recv_sem=c_recv.at[d],
            device_id={"dp": peer(d)},
            device_id_type=MESH,
        )
        for d in offsets
    ]
    for copy in c_copies:
        copy.start()

    forwards = {(d, e): forward(d, e) for d in offsets for e in range(1, tensors)}
    held = [0]
    for i, b in enumerate(bits):
        for slot in held:
            g_copies[slot + b].wait_recv()
            for later in bits[i + 1 :]:
                g_copies[slot + b + later] = g_copy(grads.at[slot + b, part(tensor)], slot + b, later)
                g_copies[slot + b + later].start()
            for e in range(1, tensors):
                forwards[slot + b, e].start()
        held = held + [slot + b for slot in held]

    for copy in c_copies:
        copy.wait()
    whole = counts[0]
    for d in offsets:
        whole = whole + counts[d]
    factor = 1.0 / whole.astype(jnp.float32)
    scale[...] = factor
    factor = factor[0:1, 0:1]

    def times(block, d):
        return lax.dot_general(
            block, grads[d], (((0,), (0,)), ((), ())), preferred_element_type=jnp.float32
        )

    mine_load.wait()
    for k in range(n_cuts):
        cut = slice(k * tile, (k + 1) * tile)
        total[cut, :] = times(mine[:, cut], 0)
    for k in range(n_cuts - ahead):
        for d in offsets:
            n_copies[d, k].wait_send()
            n_copies[d, k + ahead].start()
    for d in offsets:
        for e in range(1, tensors):
            forwards[d, e].wait_recv()
    for k in range(n_cuts - 1):
        cut = slice(k * tile, (k + 1) * tile)
        for d in reversed(offsets):
            n_copies[d, k].wait_recv()
            if d == offsets[0]:
                total[cut, :] = (total[cut, :] + times(arrived[d - 1, k], d)) * factor
            else:
                total[cut, :] += times(arrived[d - 1, k], d)

    @pl.when(pipe < sections - 1)
    def _():
        for c in range(x_cuts):
            x_copy(c).wait_recv()
            wide = slice(c * step, (c + 1) * step)
            passed[:, wide] = (passed[:, wide].astype(jnp.float32) * factor).astype(passed.dtype)

    @pl.when(pipe == sections - 1)
    def _():
        passed[...] = jnp.zeros(passed.shape, passed.dtype)

    @pl.when(pipe > 0)
    def _():
        for c in range(x_cuts):
            x_copy(c).wait_send()

    for d in reversed(offsets):
        n_copies[d, n_cuts - 1].wait_recv()
    for k in range(max(n_cuts - ahead, 0), n_cuts):
        for d in offsets:
            n_copies[d, k].wait_send()
    for d in offsets:
        g_copies[d].wait_send()
        for e in range(1, tensors):
            forwards[d, e].wait_send()


def finish(cuts, total, passed, grads, last, scale, grad_out, passed_out, closing, g_sem, p_sem):
    high = closing.shape[0]
    wide = passed.shape[1] // cuts
    ready = total.shape[0] - high
    copies = []
    for c in range(cuts):
        cut = pl.ds(c * wide, wide)
        copies.append(pltpu.make_async_copy(passed.at[:, cut], passed_out.at[0, :, cut], p_sem.at[c]))
    for c in range(ready // high):
        tall = pl.ds(c * high, high)
        copies.append(pltpu.make_async_copy(total.at[tall], grad_out.at[0, 0, tall], g_sem.at[c]))
    for copy in copies:
        copy.start()
    rest = total[ready:, :]
    for d in range(1, grads.shape[0]):
        rest = rest + lax.dot_general(
            last[d - 1], grads[d], (((0,), (0,)), ((), ())), preferred_element_type=jnp.float32
        )
    closing[...] = rest * scale[0:1, 0:1]
    copies.append(
        pltpu.make_async_copy(closing, grad_out.at[0, 0, pl.ds(ready, high)], g_sem.at[ready // high])
    )
    copies[-1].start()
    for copy in copies:
        copy.wait()


def in_kernels(replicas, tensors, sections, normed, w_value, grad_value, assistant_mask):
    _, rows, width = normed.shape
    heads = w_value.shape[2]
    owned = width // replicas
    x_cuts = pieces_of(width, LANES, 8)
    n_cuts = pieces_of(owned, LANES, 4)
    kind = normed.dtype
    vmem = pl.BlockSpec(memory_space=pltpu.VMEM)
    anywhere = pl.BlockSpec(memory_space=pl.ANY)
    dma = pltpu.SemaphoreType.DMA
    size = kind.itemsize
    held = size * (rows * owned * replicas + replicas * rows * heads + width * heads + rows * width)
    held += 4 * assistant_mask.size
    arguments = [
        pltpu.with_memory_space_constraint(array, pltpu.HBM)
        for array in (normed, w_value, grad_value, assistant_mask)
    ]
    results = pl.pallas_call(
        functools.partial(exchange, replicas, tensors, sections, x_cuts, n_cuts),
        out_shape=(
            pltpu.VMEM((owned, heads), jnp.float32),
            pltpu.VMEM((rows, width), kind),
            pltpu.VMEM((replicas, rows, heads), kind),
            pltpu.VMEM((replicas - 1, rows, owned // n_cuts), kind),
            pltpu.VMEM((8, LANES), jnp.float32),
        ),
        in_specs=[anywhere] * 4,
        out_specs=(vmem,) * 5,
        scratch_shapes=[
            pltpu.VMEM((rows, owned), kind),
            pltpu.VMEM((replicas - 1, max(n_cuts - 1, 1), rows, owned // n_cuts), kind),
            pltpu.VMEM((width, heads), kind),
            pltpu.VMEM((rows, width), kind),
            pltpu.VMEM((replicas, 8, LANES), jnp.int32),
            pltpu.VMEM(assistant_mask.shape[1:], jnp.int32),
            dma((3,)),
            dma((x_cuts,)),
            dma((replicas, n_cuts)),
            dma((replicas, n_cuts)),
            dma((replicas,)),
            dma((replicas,)),
            dma((replicas, tensors)),
            dma((replicas, tensors)),
            dma((replicas,)),
            dma((replicas,)),
            dma((x_cuts,)),
            dma((x_cuts,)),
        ],
        compiler_params=pltpu.CompilerParams(
            collective_id=0, has_side_effects=True, vmem_limit_bytes=held + (8 << 20)
        ),
        name="exchange",
    )(*arguments)
    out_cuts = pieces_of(width, LANES, 4)
    return pl.pallas_call(
        functools.partial(finish, out_cuts),
        out_shape=(
            jax.ShapeDtypeStruct((1, 1, owned, heads), jnp.float32),
            jax.ShapeDtypeStruct((1, rows, width), kind),
        ),
        in_specs=[vmem] * 5,
        out_specs=(anywhere, anywhere),
        scratch_shapes=[
            pltpu.VMEM((owned // n_cuts, heads), jnp.float32),
            dma((n_cuts,)),
            dma((out_cuts,)),
        ],
        compiler_params=pltpu.CompilerParams(vmem_limit_bytes=4 * owned * heads + (8 << 20)),
        name="finish",
    )(*results)


def with_collectives(normed, w_value, grad_value, assistant_mask):
    local_count = jnp.sum(assistant_mask, dtype=jnp.int32)
    mask_total = lax.psum(local_count, "dp")
    divisor = mask_total.astype(jnp.float32)
    inputs = normed[0]
    weight = w_value[0]
    upstream = grad_value[0]
    local_width = inputs.shape[1]
    replicas = lax.axis_size("dp")
    padded_rows = (local_width + replicas - 1) // replicas * replicas
    padded = jnp.pad(inputs, ((0, 0), (0, padded_rows - local_width)))
    weight_sum = lax.psum_scatter(
        lax.dot_general(
            padded, upstream, (((0,), (0,)), ((), ())), preferred_element_type=jnp.float32
        ).astype(jnp.bfloat16),
        "dp",
        scatter_dimension=0,
        tiled=True,
    ).astype(jnp.float32)
    total = jnp.zeros((upstream.shape[0], local_width), jnp.float32)
    for head in range(KV_HEADS):
        piece_up = upstream[:, head * HEAD : (head + 1) * HEAD]
        piece_w = weight[:, head * HEAD : (head + 1) * HEAD]
        part = lax.dot_general(
            piece_up, piece_w, (((1,), (1,)), ((), ())), preferred_element_type=jnp.float32
        ).astype(jnp.bfloat16)
        total = total + part.astype(jnp.float32)
    weight_grad = weight_sum / divisor
    input_grad = (total / divisor).astype(jnp.bfloat16)
    passed = from_behind(input_grad, "pipe", -1)
    return (weight_grad[None, None], passed[None])


def solution(mesh):
    replicas, tensors, sections = mesh.shape["dp"], mesh.shape["tensor"], mesh.shape["pipe"]

    def local(normed, w_value, grad_value, assistant_mask):
        _, rows, width = normed.shape
        aligned = width % (replicas * LANES) == 0 and rows % (tensors * PACK) == 0
        aligned = aligned and replicas & (replicas - 1) == 0
        if aligned and min(replicas, tensors, sections) > 1:
            return in_kernels(replicas, tensors, sections, normed, w_value, grad_value, assistant_mask)
        return with_collectives(normed, w_value, grad_value, assistant_mask)

    return jax.shard_map(
        local,
        mesh=mesh,
        in_specs=(
            P("pipe", "dp", "tensor"),
            P("pipe", "tensor", None),
            P("pipe", "dp", None),
            P("dp", None, None),
        ),
        out_specs=(P("pipe", "tensor", "dp", None), P("pipe", "dp", "tensor")),
        check_vma=False,
    )
```

```python
import functools

import jax
import jax.numpy as jnp
from jax import lax
from jax.experimental import pallas as pl
from jax.experimental.pallas import tpu as pltpu
from jax.sharding import PartitionSpec as P

HEAD = 128
KV_HEADS = 8
LANES = 128
PACK = 16
MESH = pl.DeviceIdType.MESH


def from_behind(block, axis, distance):
    devices = range(lax.axis_size(axis))
    route = [(i - distance, i) for i in devices if i - distance in devices]
    return lax.ppermute(block, axis, route)


def pieces_of(extent, unit, most):
    for count in range(most, 0, -1):
        if extent % (count * unit) == 0:
            return count
    return 1


def spans_of(extent):
    unit = extent // 8
    sizes = [unit, 2 * unit, 2 * unit, 2 * unit, unit] if extent % (8 * LANES) == 0 else [extent]
    starts = [sum(sizes[:i]) for i in range(len(sizes))]
    return list(zip(starts, sizes))


def exchange(
    replicas, tensors, sections, x_cuts, spans, closing,
    normed, weight, grad, mask,
    total, passed, grads, arrived, scale,
    mine, weights, sending, counts, masks,
    load_sem, w_sem, n_send, n_recv, g_send, g_recv, f_send, f_recv, c_send, c_recv, x_send, x_recv,
):
    dp = lax.axis_index("dp")
    tensor = lax.axis_index("tensor")
    pipe = lax.axis_index("pipe")
    rows = grads.shape[1]
    share = rows // tensors
    owned = mine.shape[1]
    n_cuts = len(spans)
    step = passed.shape[1] // x_cuts
    bits = [1 << b for b in reversed(range(replicas.bit_length() - 1))]
    offsets = range(replicas - 1, 0, -1)

    def peer(d):
        return dp + sum(b * (1 - 2 * lax.rem(dp // b, 2)) for b in bits if d & b)

    def mate(e):
        return lax.rem(tensor + e, tensors)

    def part(index):
        return pl.ds(pl.multiple_of(index * share, PACK), share)

    def columns(index, k):
        return pl.ds(pl.multiple_of(index * owned + spans[k][0], LANES), spans[k][1])

    barrier = pltpu.get_barrier_semaphore()
    for d in offsets:
        pl.semaphore_signal(barrier, inc=1, device_id={"dp": peer(d)}, device_id_type=MESH)
    for e in range(1, tensors):
        pl.semaphore_signal(barrier, inc=1, device_id={"tensor": mate(e)}, device_id_type=MESH)
    pl.semaphore_signal(
        barrier, inc=1, device_id={"pipe": lax.rem(pipe + 1, sections)}, device_id_type=MESH
    )

    grad_load = pltpu.make_async_copy(grad.at[0], grads.at[0], load_sem.at[0])
    grad_load.start()
    w_loads = [
        pltpu.make_async_copy(
            weight.at[0, pl.ds(c * step, step)], weights.at[pl.ds(c * step, step)], w_sem.at[c]
        )
        for c in range(x_cuts)
    ]

    @pl.when(pipe > 0)
    def _():
        for load in w_loads:
            load.start()

    mask_load = pltpu.make_async_copy(mask.at[0], masks, load_sem.at[1])
    mask_load.start()
    mine_load = pltpu.make_async_copy(
        normed.at[0, :, pl.ds(pl.multiple_of(dp * owned, LANES), owned)], mine, load_sem.at[2]
    )
    mine_load.start()

    pl.semaphore_wait(barrier, replicas - 1 + tensors - 1 + 1)

    def g_copy(source, slot, b):
        return pltpu.make_async_remote_copy(
            src_ref=source,
            dst_ref=grads.at[slot + b, part(tensor)],
            send_sem=g_send.at[slot + b],
            recv_sem=g_recv.at[slot + b],
            device_id={"dp": peer(b)},
            device_id_type=MESH,
        )

    def n_copy(d, k):
        return pltpu.make_async_remote_copy(
            src_ref=normed.at[0, :, columns(peer(d), k)],
            dst_ref=arrived.at[d - 1, :, pl.ds(*spans[k])],
            send_sem=n_send.at[d, k],
            recv_sem=n_recv.at[d, k],
            device_id={"dp": peer(d)},
            device_id_type=MESH,
        )

    def x_copy(c):
        cut = pl.ds(c * step, step)
        return pltpu.make_async_remote_copy(
            src_ref=sending.at[:, cut],
            dst_ref=passed.at[:, cut],
            send_sem=x_send.at[c],
            recv_sem=x_recv.at[c],
            device_id={"pipe": lax.rem(pipe + sections - 1, sections)},
            device_id_type=MESH,
        )

    def forward(d, e):
        return pltpu.make_async_remote_copy(
            src_ref=grads.at[d, part(tensor)],
            dst_ref=grads.at[d, part(tensor)],
            send_sem=f_send.at[d, e],
            recv_sem=f_recv.at[d, e],
            device_id={"tensor": mate(e)},
            device_id_type=MESH,
        )

    own = grad.at[0, part(tensor)]
    g_copies = {b: g_copy(own, 0, b) for b in bits}
    for b in bits:
        g_copies[b].start()
    ahead = min(2, n_cuts)
    n_copies = {(d, k): n_copy(d, k) for d in offsets for k in range(n_cuts)}
    for k in range(ahead):
        for d in offsets:
            n_copies[d, k].start()

    grad_load.wait()

    @pl.when(pipe > 0)
    def _():
        for c in range(x_cuts):
            w_loads[c].wait()
            sending[:, c * step : (c + 1) * step] = lax.dot_general(
                grads[0],
                weights[c * step : (c + 1) * step, :],
                (((1,), (1,)), ((), ())),
                preferred_element_type=jnp.float32,
            ).astype(sending.dtype)
            x_copy(c).start()

    mask_load.wait()
    counts[0] = jnp.full(counts.shape[1:], jnp.sum(masks[...], dtype=jnp.int32), jnp.int32)
    c_copies = [
        pltpu.make_async_remote_copy(
            src_ref=counts.at[0],
            dst_ref=counts.at[d],
            send_sem=c_send.at[d],
            recv_sem=c_recv.at[d],
            device_id={"dp": peer(d)},
            device_id_type=MESH,
        )
        for d in offsets
    ]
    for copy in c_copies:
        copy.start()

    forwards = {(d, e): forward(d, e) for d in offsets for e in range(1, tensors)}
    held = [0]
    for i, b in enumerate(bits):
        for slot in held:
            g_copies[slot + b].wait_recv()
            for later in bits[i + 1 :]:
                g_copies[slot + b + later] = g_copy(grads.at[slot + b, part(tensor)], slot + b, later)
                g_copies[slot + b + later].start()
            for e in range(1, tensors):
                forwards[slot + b, e].start()
        held = held + [slot + b for slot in held]

    for copy in c_copies:
        copy.wait()
    whole = counts[0]
    for d in offsets:
        whole = whole + counts[d]
    factor = 1.0 / whole.astype(jnp.float32)
    scale[...] = factor
    factor = factor[0:1, 0:1]

    def times(block, d):
        return lax.dot_general(
            block, grads[d], (((0,), (0,)), ((), ())), preferred_element_type=jnp.float32
        )

    mine_load.wait()
    for start, extent in spans:
        cut = slice(start, start + extent)
        total[cut, :] = times(mine[:, cut], 0)
    for k in range(n_cuts - ahead):
        for d in offsets:
            n_copies[d, k].wait_send()
            n_copies[d, k + ahead].start()
    for d in offsets:
        for e in range(1, tensors):
            forwards[d, e].wait_recv()
    for k in range(n_cuts - closing):
        cut = slice(spans[k][0], spans[k][0] + spans[k][1])
        for d in reversed(offsets):
            n_copies[d, k].wait_recv()
            if d == offsets[0]:
                total[cut, :] = (total[cut, :] + times(arrived[d - 1, :, cut], d)) * factor
            else:
                total[cut, :] += times(arrived[d - 1, :, cut], d)

    @pl.when(pipe < sections - 1)
    def _():
        for c in range(x_cuts):
            x_copy(c).wait_recv()
            wide = slice(c * step, (c + 1) * step)
            passed[:, wide] = (passed[:, wide].astype(jnp.float32) * factor).astype(passed.dtype)

    @pl.when(pipe == sections - 1)
    def _():
        passed[...] = jnp.zeros(passed.shape, passed.dtype)

    @pl.when(pipe > 0)
    def _():
        for c in range(x_cuts):
            x_copy(c).wait_send()

    for k in range(n_cuts - closing, n_cuts):
        for d in reversed(offsets):
            n_copies[d, k].wait_recv()
    for k in range(max(n_cuts - ahead, 0), n_cuts):
        for d in offsets:
            n_copies[d, k].wait_send()
    for d in offsets:
        g_copies[d].wait_send()
        for e in range(1, tensors):
            forwards[d, e].wait_send()


def finish(cuts, spans, total, passed, grads, arrived, scale, grad_out, passed_out, rest, g_sem, p_sem):
    ready = spans[0][0]
    wide = passed.shape[1] // cuts
    copies = []
    if ready:
        tall = pl.ds(0, ready)
        copies.append(pltpu.make_async_copy(total.at[tall], grad_out.at[0, 0, tall], g_sem.at[0]))
    for c in range(cuts):
        cut = pl.ds(c * wide, wide)
        copies.append(pltpu.make_async_copy(passed.at[:, cut], passed_out.at[0, :, cut], p_sem.at[c]))
    for copy in copies:
        copy.start()
    for k, (start, extent) in enumerate(spans):
        cut = slice(start, start + extent)
        here = pl.ds(start - ready, extent)
        part = total[cut, :]
        for d in range(1, grads.shape[0]):
            part = part + lax.dot_general(
                arrived[d - 1, :, cut], grads[d], (((0,), (0,)), ((), ())), preferred_element_type=jnp.float32
            )
        rest[here, :] = part * scale[0:1, 0:1]
        copies.append(
            pltpu.make_async_copy(
                rest.at[here], grad_out.at[0, 0, pl.ds(start, extent)], g_sem.at[k + 1]
            )
        )
        copies[-1].start()
    for copy in copies:
        copy.wait()


def in_kernels(replicas, tensors, sections, normed, w_value, grad_value, assistant_mask):
    _, rows, width = normed.shape
    heads = w_value.shape[2]
    owned = width // replicas
    x_cuts = pieces_of(width, LANES, 8)
    spans = spans_of(owned)
    closing = min(2, len(spans))
    n_cuts = len(spans)
    kind = normed.dtype
    vmem = pl.BlockSpec(memory_space=pltpu.VMEM)
    anywhere = pl.BlockSpec(memory_space=pl.ANY)
    dma = pltpu.SemaphoreType.DMA
    size = kind.itemsize
    held = size * (rows * owned * replicas + replicas * rows * heads + width * heads + rows * width)
    held += 4 * assistant_mask.size
    arguments = [
        pltpu.with_memory_space_constraint(array, pltpu.HBM)
        for array in (normed, w_value, grad_value, assistant_mask)
    ]
    results = pl.pallas_call(
        functools.partial(exchange, replicas, tensors, sections, x_cuts, spans, closing),
        out_shape=(
            pltpu.VMEM((owned, heads), jnp.float32),
            pltpu.VMEM((rows, width), kind),
            pltpu.VMEM((replicas, rows, heads), kind),
            pltpu.VMEM((replicas - 1, rows, owned), kind),
            pltpu.VMEM((8, LANES), jnp.float32),
        ),
        in_specs=[anywhere] * 4,
        out_specs=(vmem,) * 5,
        scratch_shapes=[
            pltpu.VMEM((rows, owned), kind),
            pltpu.VMEM((width, heads), kind),
            pltpu.VMEM((rows, width), kind),
            pltpu.VMEM((replicas, 8, LANES), jnp.int32),
            pltpu.VMEM(assistant_mask.shape[1:], jnp.int32),
            dma((3,)),
            dma((x_cuts,)),
            dma((replicas, n_cuts)),
            dma((replicas, n_cuts)),
            dma((replicas,)),
            dma((replicas,)),
            dma((replicas, tensors)),
            dma((replicas, tensors)),
            dma((replicas,)),
            dma((replicas,)),
            dma((x_cuts,)),
            dma((x_cuts,)),
        ],
        compiler_params=pltpu.CompilerParams(
            collective_id=0, has_side_effects=True, vmem_limit_bytes=held + (8 << 20)
        ),
        name="exchange",
    )(*arguments)
    out_cuts = pieces_of(width, LANES, 4)
    return pl.pallas_call(
        functools.partial(finish, out_cuts, spans[-closing:]),
        out_shape=(
            jax.ShapeDtypeStruct((1, 1, owned, heads), jnp.float32),
            jax.ShapeDtypeStruct((1, rows, width), kind),
        ),
        in_specs=[vmem] * 5,
        out_specs=(anywhere, anywhere),
        scratch_shapes=[
            pltpu.VMEM((owned - spans[-closing][0], heads), jnp.float32),
            dma((closing + 1,)),
            dma((out_cuts,)),
        ],
        compiler_params=pltpu.CompilerParams(vmem_limit_bytes=4 * owned * heads + (8 << 20)),
        name="finish",
    )(*results)


def with_collectives(normed, w_value, grad_value, assistant_mask):
    local_count = jnp.sum(assistant_mask, dtype=jnp.int32)
    mask_total = lax.psum(local_count, "dp")
    divisor = mask_total.astype(jnp.float32)
    inputs = normed[0]
    weight = w_value[0]
    upstream = grad_value[0]
    local_width = inputs.shape[1]
    replicas = lax.axis_size("dp")
    padded_rows = (local_width + replicas - 1) // replicas * replicas
    padded = jnp.pad(inputs, ((0, 0), (0, padded_rows - local_width)))
    weight_sum = lax.psum_scatter(
        lax.dot_general(
            padded, upstream, (((0,), (0,)), ((), ())), preferred_element_type=jnp.float32
        ).astype(jnp.bfloat16),
        "dp",
        scatter_dimension=0,
        tiled=True,
    ).astype(jnp.float32)
    total = jnp.zeros((upstream.shape[0], local_width), jnp.float32)
    for head in range(KV_HEADS):
        piece_up = upstream[:, head * HEAD : (head + 1) * HEAD]
        piece_w = weight[:, head * HEAD : (head + 1) * HEAD]
        part = lax.dot_general(
            piece_up, piece_w, (((1,), (1,)), ((), ())), preferred_element_type=jnp.float32
        ).astype(jnp.bfloat16)
        total = total + part.astype(jnp.float32)
    weight_grad = weight_sum / divisor
    input_grad = (total / divisor).astype(jnp.bfloat16)
    passed = from_behind(input_grad, "pipe", -1)
    return (weight_grad[None, None], passed[None])


def solution(mesh):
    replicas, tensors, sections = mesh.shape["dp"], mesh.shape["tensor"], mesh.shape["pipe"]

    def local(normed, w_value, grad_value, assistant_mask):
        _, rows, width = normed.shape
        aligned = width % (replicas * LANES) == 0 and rows % (tensors * PACK) == 0
        aligned = aligned and replicas & (replicas - 1) == 0
        if aligned and min(replicas, tensors, sections) > 1:
            return in_kernels(replicas, tensors, sections, normed, w_value, grad_value, assistant_mask)
        return with_collectives(normed, w_value, grad_value, assistant_mask)

    return jax.shard_map(
        local,
        mesh=mesh,
        in_specs=(
            P("pipe", "dp", "tensor"),
            P("pipe", "tensor", None),
            P("pipe", "dp", None),
            P("dp", None, None),
        ),
        out_specs=(P("pipe", "tensor", "dp", None), P("pipe", "dp", "tensor")),
        check_vma=False,
    )
```

```python
import functools

import jax
import jax.numpy as jnp
from jax import lax
from jax.experimental import pallas as pl
from jax.experimental.pallas import tpu as pltpu
from jax.sharding import PartitionSpec as P

HEAD = 128
KV_HEADS = 8
LANES = 128
PACK = 16
MESH = pl.DeviceIdType.MESH


def from_behind(block, axis, distance):
    devices = range(lax.axis_size(axis))
    route = [(i - distance, i) for i in devices if i - distance in devices]
    return lax.ppermute(block, axis, route)


def pieces_of(extent, unit, most):
    for count in range(most, 0, -1):
        if extent % (count * unit) == 0:
            return count
    return 1


def exchange(
    replicas, tensors, sections, x_cuts, n_cuts,
    normed, weight, grad, mask,
    total, passed, grads, last, scale,
    mine, arrived, weights, sending, counts, masks,
    load_sem, w_sem, n_send, n_recv, g_send, g_recv, f_send, f_recv, c_send, c_recv, x_send, x_recv,
):
    dp = lax.axis_index("dp")
    tensor = lax.axis_index("tensor")
    pipe = lax.axis_index("pipe")
    rows = grads.shape[1]
    share = rows // tensors
    owned = mine.shape[1]
    tile = owned // n_cuts
    step = passed.shape[1] // x_cuts
    bits = [1 << b for b in reversed(range(replicas.bit_length() - 1))]
    offsets = range(replicas - 1, 0, -1)

    def peer(d):
        return dp + sum(b * (1 - 2 * lax.rem(dp // b, 2)) for b in bits if d & b)

    def mate(e):
        return lax.rem(tensor + e, tensors)

    def part(index):
        return pl.ds(pl.multiple_of(index * share, PACK), share)

    def columns(index, k):
        return pl.ds(pl.multiple_of(index * owned + k * tile, LANES), tile)

    barrier = pltpu.get_barrier_semaphore()
    for d in offsets:
        pl.semaphore_signal(barrier, inc=1, device_id={"dp": peer(d)}, device_id_type=MESH)
    for e in range(1, tensors):
        pl.semaphore_signal(barrier, inc=1, device_id={"tensor": mate(e)}, device_id_type=MESH)
    pl.semaphore_signal(
        barrier, inc=1, device_id={"pipe": lax.rem(pipe + 1, sections)}, device_id_type=MESH
    )

    grad_load = pltpu.make_async_copy(grad.at[0], grads.at[0], load_sem.at[0])
    grad_load.start()
    w_loads = [
        pltpu.make_async_copy(
            weight.at[0, pl.ds(c * step, step)], weights.at[pl.ds(c * step, step)], w_sem.at[c]
        )
        for c in range(x_cuts)
    ]

    @pl.when(pipe > 0)
    def _():
        for load in w_loads:
            load.start()

    mask_load = pltpu.make_async_copy(mask.at[0], masks, load_sem.at[1])
    mask_load.start()
    mine_load = pltpu.make_async_copy(
        normed.at[0, :, pl.ds(pl.multiple_of(dp * owned, LANES), owned)], mine, load_sem.at[2]
    )
    mine_load.start()

    pl.semaphore_wait(barrier, replicas - 1 + tensors - 1 + 1)

    def g_copy(source, slot, b):
        return pltpu.make_async_remote_copy(
            src_ref=source,
            dst_ref=grads.at[slot + b, part(tensor)],
            send_sem=g_send.at[slot + b],
            recv_sem=g_recv.at[slot + b],
            device_id={"dp": peer(b)},
            device_id_type=MESH,
        )

    def n_copy(target, d, j, k):
        return pltpu.make_async_remote_copy(
            src_ref=normed.at[0, :, columns(target, k)],
            dst_ref=last.at[d - 1] if k == n_cuts - 1 else arrived.at[d - 1, k],
            send_sem=n_send.at[j, k],
            recv_sem=n_recv.at[d, k],
            device_id={"dp": target},
            device_id_type=MESH,
        )

    def x_copy(c):
        cut = pl.ds(c * step, step)
        return pltpu.make_async_remote_copy(
            src_ref=sending.at[:, cut],
            dst_ref=passed.at[:, cut],
            send_sem=x_send.at[c],
            recv_sem=x_recv.at[c],
            device_id={"pipe": lax.rem(pipe + sections - 1, sections)},
            device_id_type=MESH,
        )

    def forward(d, e):
        return pltpu.make_async_remote_copy(
            src_ref=grads.at[d, part(tensor)],
            dst_ref=grads.at[d, part(tensor)],
            send_sem=f_send.at[d, e],
            recv_sem=f_recv.at[d, e],
            device_id={"tensor": mate(e)},
            device_id_type=MESH,
        )

    own = grad.at[0, part(tensor)]
    g_copies = {b: g_copy(own, 0, b) for b in bits}
    for b in bits:
        g_copies[b].start()
    ahead = min(2, n_cuts)
    half = replicas // 2
    upper = dp // half
    targets = []
    for i in range(half):
        target = i * upper + (replicas - 1 - i) * (1 - upper)
        targets.append((target, sum(b * lax.rem(dp // b + target // b, 2) for b in bits)))
    targets += [(peer(d), d) for d in range(1, half)]
    window = [n_cuts] + [ahead] * (len(targets) - 1)
    sends = {(j, k): n_copy(*targets[j], j, k) for j in range(len(targets)) for k in range(n_cuts)}
    n_copies = {(d, k): n_copy(peer(d), d, d - 1, k) for d in offsets for k in range(n_cuts)}
    for k in range(n_cuts):
        for j in range(len(targets)):
            if k < window[j]:
                sends[j, k].start()

    grad_load.wait()

    @pl.when(pipe > 0)
    def _():
        for c in range(x_cuts):
            w_loads[c].wait()
            sending[:, c * step : (c + 1) * step] = lax.dot_general(
                grads[0],
                weights[c * step : (c + 1) * step, :],
                (((1,), (1,)), ((), ())),
                preferred_element_type=jnp.float32,
            ).astype(sending.dtype)
            x_copy(c).start()

    mask_load.wait()
    counts[0] = jnp.full(counts.shape[1:], jnp.sum(masks[...], dtype=jnp.int32), jnp.int32)
    c_copies = [
        pltpu.make_async_remote_copy(
            src_ref=counts.at[0],
            dst_ref=counts.at[d],
            send_sem=c_send.at[d],
            recv_sem=c_recv.at[d],
            device_id={"dp": peer(d)},
            device_id_type=MESH,
        )
        for d in offsets
    ]
    for copy in c_copies:
        copy.start()

    forwards = {(d, e): forward(d, e) for d in offsets for e in range(1, tensors)}
    held = [0]
    for i, b in enumerate(bits):
        for slot in held:
            g_copies[slot + b].wait_recv()
            for later in bits[i + 1 :]:
                g_copies[slot + b + later] = g_copy(grads.at[slot + b, part(tensor)], slot + b, later)
                g_copies[slot + b + later].start()
            for e in range(1, tensors):
                forwards[slot + b, e].start()
        held = held + [slot + b for slot in held]

    for copy in c_copies:
        copy.wait()
    whole = counts[0]
    for d in offsets:
        whole = whole + counts[d]
    factor = 1.0 / whole.astype(jnp.float32)
    scale[...] = factor
    factor = factor[0:1, 0:1]

    def times(block, d):
        return lax.dot_general(
            block, grads[d], (((0,), (0,)), ((), ())), preferred_element_type=jnp.float32
        )

    mine_load.wait()
    for k in range(n_cuts):
        cut = slice(k * tile, (k + 1) * tile)
        total[cut, :] = times(mine[:, cut], 0)
    for k in range(n_cuts - ahead):
        for j in range(1, len(targets)):
            sends[j, k].wait_send()
            sends[j, k + ahead].start()
    for d in offsets:
        for e in range(1, tensors):
            forwards[d, e].wait_recv()
    for k in range(n_cuts - 1):
        cut = slice(k * tile, (k + 1) * tile)
        for d in reversed(offsets):
            n_copies[d, k].wait_recv()
            if d == offsets[0]:
                total[cut, :] = (total[cut, :] + times(arrived[d - 1, k], d)) * factor
            else:
                total[cut, :] += times(arrived[d - 1, k], d)

    @pl.when(pipe < sections - 1)
    def _():
        for c in range(x_cuts):
            x_copy(c).wait_recv()
            wide = slice(c * step, (c + 1) * step)
            passed[:, wide] = (passed[:, wide].astype(jnp.float32) * factor).astype(passed.dtype)

    @pl.when(pipe == sections - 1)
    def _():
        passed[...] = jnp.zeros(passed.shape, passed.dtype)

    @pl.when(pipe > 0)
    def _():
        for c in range(x_cuts):
            x_copy(c).wait_send()

    for d in reversed(offsets):
        n_copies[d, n_cuts - 1].wait_recv()
    for j in range(len(targets)):
        for k in range(n_cuts - window[j], n_cuts):
            sends[j, k].wait_send()
    for d in offsets:
        g_copies[d].wait_send()
        for e in range(1, tensors):
            forwards[d, e].wait_send()


def finish(cuts, total, passed, grads, last, scale, grad_out, passed_out, closing, g_sem, p_sem):
    high = closing.shape[0]
    wide = passed.shape[1] // cuts
    ready = total.shape[0] - high
    copies = []
    for c in range(cuts):
        cut = pl.ds(c * wide, wide)
        copies.append(pltpu.make_async_copy(passed.at[:, cut], passed_out.at[0, :, cut], p_sem.at[c]))
    for c in range(ready // high):
        tall = pl.ds(c * high, high)
        copies.append(pltpu.make_async_copy(total.at[tall], grad_out.at[0, 0, tall], g_sem.at[c]))
    for copy in copies:
        copy.start()
    rest = total[ready:, :]
    for d in range(1, grads.shape[0]):
        rest = rest + lax.dot_general(
            last[d - 1], grads[d], (((0,), (0,)), ((), ())), preferred_element_type=jnp.float32
        )
    closing[...] = rest * scale[0:1, 0:1]
    copies.append(
        pltpu.make_async_copy(closing, grad_out.at[0, 0, pl.ds(ready, high)], g_sem.at[ready // high])
    )
    copies[-1].start()
    for copy in copies:
        copy.wait()


def in_kernels(replicas, tensors, sections, normed, w_value, grad_value, assistant_mask):
    _, rows, width = normed.shape
    heads = w_value.shape[2]
    owned = width // replicas
    x_cuts = pieces_of(width, LANES, 8)
    n_cuts = pieces_of(owned, LANES, 4)
    kind = normed.dtype
    vmem = pl.BlockSpec(memory_space=pltpu.VMEM)
    anywhere = pl.BlockSpec(memory_space=pl.ANY)
    dma = pltpu.SemaphoreType.DMA
    size = kind.itemsize
    held = size * (rows * owned * replicas + replicas * rows * heads + width * heads + rows * width)
    held += 4 * assistant_mask.size
    arguments = [
        pltpu.with_memory_space_constraint(array, pltpu.HBM)
        for array in (normed, w_value, grad_value, assistant_mask)
    ]
    results = pl.pallas_call(
        functools.partial(exchange, replicas, tensors, sections, x_cuts, n_cuts),
        out_shape=(
            pltpu.VMEM((owned, heads), jnp.float32),
            pltpu.VMEM((rows, width), kind),
            pltpu.VMEM((replicas, rows, heads), kind),
            pltpu.VMEM((replicas - 1, rows, owned // n_cuts), kind),
            pltpu.VMEM((8, LANES), jnp.float32),
        ),
        in_specs=[anywhere] * 4,
        out_specs=(vmem,) * 5,
        scratch_shapes=[
            pltpu.VMEM((rows, owned), kind),
            pltpu.VMEM((replicas - 1, max(n_cuts - 1, 1), rows, owned // n_cuts), kind),
            pltpu.VMEM((width, heads), kind),
            pltpu.VMEM((rows, width), kind),
            pltpu.VMEM((replicas, 8, LANES), jnp.int32),
            pltpu.VMEM(assistant_mask.shape[1:], jnp.int32),
            dma((3,)),
            dma((x_cuts,)),
            dma((replicas, n_cuts)),
            dma((replicas, n_cuts)),
            dma((replicas,)),
            dma((replicas,)),
            dma((replicas, tensors)),
            dma((replicas, tensors)),
            dma((replicas,)),
            dma((replicas,)),
            dma((x_cuts,)),
            dma((x_cuts,)),
        ],
        compiler_params=pltpu.CompilerParams(
            collective_id=0, has_side_effects=True, vmem_limit_bytes=held + (8 << 20)
        ),
        name="exchange",
    )(*arguments)
    out_cuts = pieces_of(width, LANES, 4)
    return pl.pallas_call(
        functools.partial(finish, out_cuts),
        out_shape=(
            jax.ShapeDtypeStruct((1, 1, owned, heads), jnp.float32),
            jax.ShapeDtypeStruct((1, rows, width), kind),
        ),
        in_specs=[vmem] * 5,
        out_specs=(anywhere, anywhere),
        scratch_shapes=[
            pltpu.VMEM((owned // n_cuts, heads), jnp.float32),
            dma((n_cuts,)),
            dma((out_cuts,)),
        ],
        compiler_params=pltpu.CompilerParams(vmem_limit_bytes=4 * owned * heads + (8 << 20)),
        name="finish",
    )(*results)


def with_collectives(normed, w_value, grad_value, assistant_mask):
    local_count = jnp.sum(assistant_mask, dtype=jnp.int32)
    mask_total = lax.psum(local_count, "dp")
    divisor = mask_total.astype(jnp.float32)
    inputs = normed[0]
    weight = w_value[0]
    upstream = grad_value[0]
    local_width = inputs.shape[1]
    replicas = lax.axis_size("dp")
    padded_rows = (local_width + replicas - 1) // replicas * replicas
    padded = jnp.pad(inputs, ((0, 0), (0, padded_rows - local_width)))
    weight_sum = lax.psum_scatter(
        lax.dot_general(
            padded, upstream, (((0,), (0,)), ((), ())), preferred_element_type=jnp.float32
        ).astype(jnp.bfloat16),
        "dp",
        scatter_dimension=0,
        tiled=True,
    ).astype(jnp.float32)
    total = jnp.zeros((upstream.shape[0], local_width), jnp.float32)
    for head in range(KV_HEADS):
        piece_up = upstream[:, head * HEAD : (head + 1) * HEAD]
        piece_w = weight[:, head * HEAD : (head + 1) * HEAD]
        part = lax.dot_general(
            piece_up, piece_w, (((1,), (1,)), ((), ())), preferred_element_type=jnp.float32
        ).astype(jnp.bfloat16)
        total = total + part.astype(jnp.float32)
    weight_grad = weight_sum / divisor
    input_grad = (total / divisor).astype(jnp.bfloat16)
    passed = from_behind(input_grad, "pipe", -1)
    return (weight_grad[None, None], passed[None])


def solution(mesh):
    replicas, tensors, sections = mesh.shape["dp"], mesh.shape["tensor"], mesh.shape["pipe"]

    def local(normed, w_value, grad_value, assistant_mask):
        _, rows, width = normed.shape
        aligned = width % (replicas * LANES) == 0 and rows % (tensors * PACK) == 0
        aligned = aligned and replicas & (replicas - 1) == 0
        if aligned and min(replicas, tensors, sections) > 1:
            return in_kernels(replicas, tensors, sections, normed, w_value, grad_value, assistant_mask)
        return with_collectives(normed, w_value, grad_value, assistant_mask)

    return jax.shard_map(
        local,
        mesh=mesh,
        in_specs=(
            P("pipe", "dp", "tensor"),
            P("pipe", "tensor", None),
            P("pipe", "dp", None),
            P("dp", None, None),
        ),
        out_specs=(P("pipe", "tensor", "dp", None), P("pipe", "dp", "tensor")),
        check_vma=False,
    )
```

```python
import functools

import jax
import jax.numpy as jnp
from jax import lax
from jax.experimental import pallas as pl
from jax.experimental.pallas import tpu as pltpu
from jax.sharding import PartitionSpec as P

HEAD = 128
KV_HEADS = 8
LANES = 128
PACK = 16
MESH = pl.DeviceIdType.MESH


def from_behind(block, axis, distance):
    devices = range(lax.axis_size(axis))
    route = [(i - distance, i) for i in devices if i - distance in devices]
    return lax.ppermute(block, axis, route)


def pieces_of(extent, unit, most):
    for count in range(most, 0, -1):
        if extent % (count * unit) == 0:
            return count
    return 1


def exchange(
    replicas, tensors, sections, x_cuts, n_cuts, closing,
    normed, weight, grad, mask,
    total, passed, grads, last, scale,
    mine, arrived, weights, sending, counts, masks,
    load_sem, w_sem, n_send, n_recv, g_send, g_recv, f_send, f_recv, c_send, c_recv, x_send, x_recv,
):
    dp = lax.axis_index("dp")
    tensor = lax.axis_index("tensor")
    pipe = lax.axis_index("pipe")
    rows = grads.shape[1]
    share = rows // tensors
    owned = mine.shape[1]
    tile = owned // n_cuts
    early = n_cuts - closing
    step = passed.shape[1] // x_cuts
    bits = [1 << b for b in reversed(range(replicas.bit_length() - 1))]
    offsets = range(replicas - 1, 0, -1)

    def peer(d):
        return dp + sum(b * (1 - 2 * lax.rem(dp // b, 2)) for b in bits if d & b)

    def mate(e):
        return lax.rem(tensor + e, tensors)

    def part(index):
        return pl.ds(pl.multiple_of(index * share, PACK), share)

    def columns(index, k):
        return pl.ds(pl.multiple_of(index * owned + k * tile, LANES), tile)

    barrier = pltpu.get_barrier_semaphore()
    for d in offsets:
        pl.semaphore_signal(barrier, inc=1, device_id={"dp": peer(d)}, device_id_type=MESH)
    for e in range(1, tensors):
        pl.semaphore_signal(barrier, inc=1, device_id={"tensor": mate(e)}, device_id_type=MESH)
    pl.semaphore_signal(
        barrier, inc=1, device_id={"pipe": lax.rem(pipe + 1, sections)}, device_id_type=MESH
    )

    grad_load = pltpu.make_async_copy(grad.at[0], grads.at[0], load_sem.at[0])
    grad_load.start()
    w_loads = [
        pltpu.make_async_copy(
            weight.at[0, pl.ds(c * step, step)], weights.at[pl.ds(c * step, step)], w_sem.at[c]
        )
        for c in range(x_cuts)
    ]

    @pl.when(pipe > 0)
    def _():
        for load in w_loads:
            load.start()

    mask_load = pltpu.make_async_copy(mask.at[0], masks, load_sem.at[1])
    mask_load.start()
    mine_load = pltpu.make_async_copy(
        normed.at[0, :, pl.ds(pl.multiple_of(dp * owned, LANES), owned)], mine, load_sem.at[2]
    )
    mine_load.start()

    pl.semaphore_wait(barrier, replicas - 1 + tensors - 1 + 1)

    def g_copy(source, slot, b):
        return pltpu.make_async_remote_copy(
            src_ref=source,
            dst_ref=grads.at[slot + b, part(tensor)],
            send_sem=g_send.at[slot + b],
            recv_sem=g_recv.at[slot + b],
            device_id={"dp": peer(b)},
            device_id_type=MESH,
        )

    def n_copy(target, d, j, k):
        return pltpu.make_async_remote_copy(
            src_ref=normed.at[0, :, columns(target, k)],
            dst_ref=last.at[d - 1, k - early] if k >= early else arrived.at[d - 1, k],
            send_sem=n_send.at[j, k],
            recv_sem=n_recv.at[d, k],
            device_id={"dp": target},
            device_id_type=MESH,
        )

    def x_copy(c):
        cut = pl.ds(c * step, step)
        return pltpu.make_async_remote_copy(
            src_ref=sending.at[:, cut],
            dst_ref=passed.at[:, cut],
            send_sem=x_send.at[c],
            recv_sem=x_recv.at[c],
            device_id={"pipe": lax.rem(pipe + sections - 1, sections)},
            device_id_type=MESH,
        )

    def forward(d, e):
        return pltpu.make_async_remote_copy(
            src_ref=grads.at[d, part(tensor)],
            dst_ref=grads.at[d, part(tensor)],
            send_sem=f_send.at[d, e],
            recv_sem=f_recv.at[d, e],
            device_id={"tensor": mate(e)},
            device_id_type=MESH,
        )

    own = grad.at[0, part(tensor)]
    g_copies = {b: g_copy(own, 0, b) for b in bits}
    for b in bits:
        g_copies[b].start()
    ahead = min(3, n_cuts)
    half = replicas // 2
    upper = dp // half
    targets = []
    for i in range(half):
        target = i * upper + (replicas - 1 - i) * (1 - upper)
        targets.append((target, sum(b * lax.rem(dp // b + target // b, 2) for b in bits)))
    targets += [(peer(d), d) for d in range(1, half)]
    window = [n_cuts] + [ahead] * (len(targets) - 1)
    sends = {(j, k): n_copy(*targets[j], j, k) for j in range(len(targets)) for k in range(n_cuts)}
    n_copies = {(d, k): n_copy(peer(d), d, d - 1, k) for d in offsets for k in range(n_cuts)}
    for k in range(n_cuts):
        for j in range(len(targets)):
            if k < window[j]:
                sends[j, k].start()

    grad_load.wait()

    @pl.when(pipe > 0)
    def _():
        for c in range(x_cuts):
            w_loads[c].wait()
            sending[:, c * step : (c + 1) * step] = lax.dot_general(
                grads[0],
                weights[c * step : (c + 1) * step, :],
                (((1,), (1,)), ((), ())),
                preferred_element_type=jnp.float32,
            ).astype(sending.dtype)
            x_copy(c).start()

    mask_load.wait()
    counts[0] = jnp.full(counts.shape[1:], jnp.sum(masks[...], dtype=jnp.int32), jnp.int32)
    c_copies = [
        pltpu.make_async_remote_copy(
            src_ref=counts.at[0],
            dst_ref=counts.at[d],
            send_sem=c_send.at[d],
            recv_sem=c_recv.at[d],
            device_id={"dp": peer(d)},
            device_id_type=MESH,
        )
        for d in offsets
    ]
    for copy in c_copies:
        copy.start()

    forwards = {(d, e): forward(d, e) for d in offsets for e in range(1, tensors)}
    held = [0]
    for i, b in enumerate(bits):
        for slot in held:
            g_copies[slot + b].wait_recv()
            for later in bits[i + 1 :]:
                g_copies[slot + b + later] = g_copy(grads.at[slot + b, part(tensor)], slot + b, later)
                g_copies[slot + b + later].start()
            for e in range(1, tensors):
                forwards[slot + b, e].start()
        held = held + [slot + b for slot in held]

    for copy in c_copies:
        copy.wait()
    whole = counts[0]
    for d in offsets:
        whole = whole + counts[d]
    factor = 1.0 / whole.astype(jnp.float32)
    scale[...] = factor
    factor = factor[0:1, 0:1]

    def times(block, d):
        return lax.dot_general(
            block, grads[d], (((0,), (0,)), ((), ())), preferred_element_type=jnp.float32
        )

    mine_load.wait()
    for k in range(n_cuts):
        cut = slice(k * tile, (k + 1) * tile)
        total[cut, :] = times(mine[:, cut], 0)
    for k in range(n_cuts - ahead):
        for j in range(1, len(targets)):
            sends[j, k].wait_send()
            sends[j, k + ahead].start()
    for d in offsets:
        for e in range(1, tensors):
            forwards[d, e].wait_recv()
    for k in range(early):
        cut = slice(k * tile, (k + 1) * tile)
        for d in reversed(offsets):
            n_copies[d, k].wait_recv()
            if d == offsets[0]:
                total[cut, :] = (total[cut, :] + times(arrived[d - 1, k], d)) * factor
            else:
                total[cut, :] += times(arrived[d - 1, k], d)

    @pl.when(pipe < sections - 1)
    def _():
        for c in range(x_cuts):
            x_copy(c).wait_recv()
            wide = slice(c * step, (c + 1) * step)
            passed[:, wide] = (passed[:, wide].astype(jnp.float32) * factor).astype(passed.dtype)

    @pl.when(pipe == sections - 1)
    def _():
        passed[...] = jnp.zeros(passed.shape, passed.dtype)

    @pl.when(pipe > 0)
    def _():
        for c in range(x_cuts):
            x_copy(c).wait_send()

    for k in range(early, n_cuts):
        for d in reversed(offsets):
            n_copies[d, k].wait_recv()
    for j in range(len(targets)):
        for k in range(n_cuts - window[j], n_cuts):
            sends[j, k].wait_send()
    for d in offsets:
        g_copies[d].wait_send()
        for e in range(1, tensors):
            forwards[d, e].wait_send()


def finish(cuts, closing, total, passed, grads, last, scale, grad_out, passed_out, rest, g_sem, p_sem):
    high = rest.shape[0] // closing
    wide = passed.shape[1] // cuts
    early = total.shape[0] // high - closing
    copies = []
    for c in range(early):
        tall = pl.ds(c * high, high)
        copies.append(pltpu.make_async_copy(total.at[tall], grad_out.at[0, 0, tall], g_sem.at[c]))
    for c in range(cuts):
        cut = pl.ds(c * wide, wide)
        copies.append(pltpu.make_async_copy(passed.at[:, cut], passed_out.at[0, :, cut], p_sem.at[c]))
    for copy in copies:
        copy.start()
    for k in range(closing):
        c = early + k
        part = total[c * high : (c + 1) * high, :]
        for d in range(1, grads.shape[0]):
            part = part + lax.dot_general(
                last[d - 1, k], grads[d], (((0,), (0,)), ((), ())), preferred_element_type=jnp.float32
            )
        rest[k * high : (k + 1) * high, :] = part * scale[0:1, 0:1]
        copies.append(
            pltpu.make_async_copy(
                rest.at[pl.ds(k * high, high)], grad_out.at[0, 0, pl.ds(c * high, high)], g_sem.at[c]
            )
        )
        copies[-1].start()
    for copy in copies:
        copy.wait()


def in_kernels(replicas, tensors, sections, normed, w_value, grad_value, assistant_mask):
    _, rows, width = normed.shape
    heads = w_value.shape[2]
    owned = width // replicas
    x_cuts = pieces_of(width, LANES, 8)
    n_cuts = pieces_of(owned, LANES, 4)
    closing = min(2, n_cuts)
    kind = normed.dtype
    vmem = pl.BlockSpec(memory_space=pltpu.VMEM)
    anywhere = pl.BlockSpec(memory_space=pl.ANY)
    dma = pltpu.SemaphoreType.DMA
    size = kind.itemsize
    held = size * (rows * owned * replicas + replicas * rows * heads + width * heads + rows * width)
    held += 4 * assistant_mask.size
    arguments = [
        pltpu.with_memory_space_constraint(array, pltpu.HBM)
        for array in (normed, w_value, grad_value, assistant_mask)
    ]
    results = pl.pallas_call(
        functools.partial(exchange, replicas, tensors, sections, x_cuts, n_cuts, closing),
        out_shape=(
            pltpu.VMEM((owned, heads), jnp.float32),
            pltpu.VMEM((rows, width), kind),
            pltpu.VMEM((replicas, rows, heads), kind),
            pltpu.VMEM((replicas - 1, closing, rows, owned // n_cuts), kind),
            pltpu.VMEM((8, LANES), jnp.float32),
        ),
        in_specs=[anywhere] * 4,
        out_specs=(vmem,) * 5,
        scratch_shapes=[
            pltpu.VMEM((rows, owned), kind),
            pltpu.VMEM((replicas - 1, max(n_cuts - closing, 1), rows, owned // n_cuts), kind),
            pltpu.VMEM((width, heads), kind),
            pltpu.VMEM((rows, width), kind),
            pltpu.VMEM((replicas, 8, LANES), jnp.int32),
            pltpu.VMEM(assistant_mask.shape[1:], jnp.int32),
            dma((3,)),
            dma((x_cuts,)),
            dma((replicas, n_cuts)),
            dma((replicas, n_cuts)),
            dma((replicas,)),
            dma((replicas,)),
            dma((replicas, tensors)),
            dma((replicas, tensors)),
            dma((replicas,)),
            dma((replicas,)),
            dma((x_cuts,)),
            dma((x_cuts,)),
        ],
        compiler_params=pltpu.CompilerParams(
            collective_id=0, has_side_effects=True, vmem_limit_bytes=held + (8 << 20)
        ),
        name="exchange",
    )(*arguments)
    out_cuts = pieces_of(width, LANES, 4)
    return pl.pallas_call(
        functools.partial(finish, out_cuts, closing),
        out_shape=(
            jax.ShapeDtypeStruct((1, 1, owned, heads), jnp.float32),
            jax.ShapeDtypeStruct((1, rows, width), kind),
        ),
        in_specs=[vmem] * 5,
        out_specs=(anywhere, anywhere),
        scratch_shapes=[
            pltpu.VMEM((closing * (owned // n_cuts), heads), jnp.float32),
            dma((n_cuts,)),
            dma((out_cuts,)),
        ],
        compiler_params=pltpu.CompilerParams(vmem_limit_bytes=4 * owned * heads + (8 << 20)),
        name="finish",
    )(*results)


def with_collectives(normed, w_value, grad_value, assistant_mask):
    local_count = jnp.sum(assistant_mask, dtype=jnp.int32)
    mask_total = lax.psum(local_count, "dp")
    divisor = mask_total.astype(jnp.float32)
    inputs = normed[0]
    weight = w_value[0]
    upstream = grad_value[0]
    local_width = inputs.shape[1]
    replicas = lax.axis_size("dp")
    padded_rows = (local_width + replicas - 1) // replicas * replicas
    padded = jnp.pad(inputs, ((0, 0), (0, padded_rows - local_width)))
    weight_sum = lax.psum_scatter(
        lax.dot_general(
            padded, upstream, (((0,), (0,)), ((), ())), preferred_element_type=jnp.float32
        ).astype(jnp.bfloat16),
        "dp",
        scatter_dimension=0,
        tiled=True,
    ).astype(jnp.float32)
    total = jnp.zeros((upstream.shape[0], local_width), jnp.float32)
    for head in range(KV_HEADS):
        piece_up = upstream[:, head * HEAD : (head + 1) * HEAD]
        piece_w = weight[:, head * HEAD : (head + 1) * HEAD]
        part = lax.dot_general(
            piece_up, piece_w, (((1,), (1,)), ((), ())), preferred_element_type=jnp.float32
        ).astype(jnp.bfloat16)
        total = total + part.astype(jnp.float32)
    weight_grad = weight_sum / divisor
    input_grad = (total / divisor).astype(jnp.bfloat16)
    passed = from_behind(input_grad, "pipe", -1)
    return (weight_grad[None, None], passed[None])


def solution(mesh):
    replicas, tensors, sections = mesh.shape["dp"], mesh.shape["tensor"], mesh.shape["pipe"]

    def local(normed, w_value, grad_value, assistant_mask):
        _, rows, width = normed.shape
        aligned = width % (replicas * LANES) == 0 and rows % (tensors * PACK) == 0
        aligned = aligned and replicas & (replicas - 1) == 0
        if aligned and min(replicas, tensors, sections) > 1:
            return in_kernels(replicas, tensors, sections, normed, w_value, grad_value, assistant_mask)
        return with_collectives(normed, w_value, grad_value, assistant_mask)

    return jax.shard_map(
        local,
        mesh=mesh,
        in_specs=(
            P("pipe", "dp", "tensor"),
            P("pipe", "tensor", None),
            P("pipe", "dp", None),
            P("dp", None, None),
        ),
        out_specs=(P("pipe", "tensor", "dp", None), P("pipe", "dp", "tensor")),
        check_vma=False,
    )
```

```python
import functools

import jax
import jax.numpy as jnp
from jax import lax
from jax.experimental import pallas as pl
from jax.experimental.pallas import tpu as pltpu
from jax.sharding import PartitionSpec as P

HEAD = 128
KV_HEADS = 8
LANES = 128
PACK = 16
MESH = pl.DeviceIdType.MESH


def from_behind(block, axis, distance):
    devices = range(lax.axis_size(axis))
    route = [(i - distance, i) for i in devices if i - distance in devices]
    return lax.ppermute(block, axis, route)


def pieces_of(extent, unit, most):
    for count in range(most, 0, -1):
        if extent % (count * unit) == 0:
            return count
    return 1


def exchange(
    replicas, tensors, sections, x_cuts, n_cuts,
    normed, weight, grad, mask,
    total, passed, grads, last, scale,
    mine, arrived, weights, sending, counts, masks,
    load_sem, w_sem, n_send, n_recv, g_send, g_recv, f_send, f_recv, c_send, c_recv, x_send, x_recv,
):
    dp = lax.axis_index("dp")
    tensor = lax.axis_index("tensor")
    pipe = lax.axis_index("pipe")
    rows = grads.shape[1]
    share = rows // tensors
    owned = mine.shape[1]
    tile = owned // n_cuts
    step = passed.shape[1] // x_cuts
    bits = [1 << b for b in reversed(range(replicas.bit_length() - 1))]
    offsets = range(replicas - 1, 0, -1)

    def peer(d):
        return dp + sum(b * (1 - 2 * lax.rem(dp // b, 2)) for b in bits if d & b)

    def mate(e):
        return lax.rem(tensor + e, tensors)

    def part(index):
        return pl.ds(pl.multiple_of(index * share, PACK), share)

    def columns(index, k):
        return pl.ds(pl.multiple_of(index * owned + k * tile, LANES), tile)

    barrier = pltpu.get_barrier_semaphore()
    for d in offsets:
        pl.semaphore_signal(barrier, inc=1, device_id={"dp": peer(d)}, device_id_type=MESH)
    for e in range(1, tensors):
        pl.semaphore_signal(barrier, inc=1, device_id={"tensor": mate(e)}, device_id_type=MESH)
    pl.semaphore_signal(
        barrier, inc=1, device_id={"pipe": lax.rem(pipe + 1, sections)}, device_id_type=MESH
    )

    grad_load = pltpu.make_async_copy(grad.at[0], grads.at[0], load_sem.at[0])
    grad_load.start()
    w_loads = [
        pltpu.make_async_copy(
            weight.at[0, pl.ds(c * step, step)], weights.at[pl.ds(c * step, step)], w_sem.at[c]
        )
        for c in range(x_cuts)
    ]

    @pl.when(pipe > 0)
    def _():
        for load in w_loads:
            load.start()

    mask_load = pltpu.make_async_copy(mask.at[0], masks, load_sem.at[1])
    mask_load.start()
    mine_load = pltpu.make_async_copy(
        normed.at[0, :, pl.ds(pl.multiple_of(dp * owned, LANES), owned)], mine, load_sem.at[2]
    )
    mine_load.start()

    pl.semaphore_wait(barrier, replicas - 1 + tensors - 1 + 1)

    def g_copy(source, slot, b):
        return pltpu.make_async_remote_copy(
            src_ref=source,
            dst_ref=grads.at[slot + b, part(tensor)],
            send_sem=g_send.at[slot + b],
            recv_sem=g_recv.at[slot + b],
            device_id={"dp": peer(b)},
            device_id_type=MESH,
        )

    def n_copy(target, d, j, k):
        return pltpu.make_async_remote_copy(
            src_ref=normed.at[0, :, columns(target, k)],
            dst_ref=last.at[d - 1] if k == n_cuts - 1 else arrived.at[d - 1, k],
            send_sem=n_send.at[j, k],
            recv_sem=n_recv.at[d, k],
            device_id={"dp": target},
            device_id_type=MESH,
        )

    def x_copy(c):
        cut = pl.ds(c * step, step)
        return pltpu.make_async_remote_copy(
            src_ref=sending.at[:, cut],
            dst_ref=passed.at[:, cut],
            send_sem=x_send.at[c],
            recv_sem=x_recv.at[c],
            device_id={"pipe": lax.rem(pipe + sections - 1, sections)},
            device_id_type=MESH,
        )

    def forward(d, e):
        return pltpu.make_async_remote_copy(
            src_ref=grads.at[d, part(tensor)],
            dst_ref=grads.at[d, part(tensor)],
            send_sem=f_send.at[d, e],
            recv_sem=f_recv.at[d, e],
            device_id={"tensor": mate(e)},
            device_id_type=MESH,
        )

    own = grad.at[0, part(tensor)]
    g_copies = {b: g_copy(own, 0, b) for b in bits}
    for b in bits:
        g_copies[b].start()
    ahead = min(2, n_cuts)
    half = replicas // 2
    upper = dp // half
    targets = []
    for i in range(half):
        target = i * upper + (replicas - 1 - i) * (1 - upper)
        targets.append((target, sum(b * lax.rem(dp // b + target // b, 2) for b in bits)))
    targets += [(peer(d), d) for d in range(1, half)]
    window = [n_cuts] + [ahead] * (half - 1) + [1] * (half - 1)
    sends = {(j, k): n_copy(*targets[j], j, k) for j in range(len(targets)) for k in range(n_cuts)}
    n_copies = {(d, k): n_copy(peer(d), d, d - 1, k) for d in offsets for k in range(n_cuts)}
    for k in range(n_cuts):
        for j in range(len(targets)):
            if k < window[j]:
                sends[j, k].start()

    grad_load.wait()

    @pl.when(pipe > 0)
    def _():
        for c in range(x_cuts):
            w_loads[c].wait()
            sending[:, c * step : (c + 1) * step] = lax.dot_general(
                grads[0],
                weights[c * step : (c + 1) * step, :],
                (((1,), (1,)), ((), ())),
                preferred_element_type=jnp.float32,
            ).astype(sending.dtype)
            x_copy(c).start()

    mask_load.wait()
    counts[0] = jnp.full(counts.shape[1:], jnp.sum(masks[...], dtype=jnp.int32), jnp.int32)
    c_copies = [
        pltpu.make_async_remote_copy(
            src_ref=counts.at[0],
            dst_ref=counts.at[d],
            send_sem=c_send.at[d],
            recv_sem=c_recv.at[d],
            device_id={"dp": peer(d)},
            device_id_type=MESH,
        )
        for d in offsets
    ]
    for copy in c_copies:
        copy.start()

    forwards = {(d, e): forward(d, e) for d in offsets for e in range(1, tensors)}
    held = [0]
    for i, b in enumerate(bits):
        for slot in held:
            g_copies[slot + b].wait_recv()
            for later in bits[i + 1 :]:
                g_copies[slot + b + later] = g_copy(grads.at[slot + b, part(tensor)], slot + b, later)
                g_copies[slot + b + later].start()
            for e in range(1, tensors):
                forwards[slot + b, e].start()
        held = held + [slot + b for slot in held]

    for copy in c_copies:
        copy.wait()
    whole = counts[0]
    for d in offsets:
        whole = whole + counts[d]
    factor = 1.0 / whole.astype(jnp.float32)
    scale[...] = factor
    factor = factor[0:1, 0:1]

    def times(block, d):
        return lax.dot_general(
            block, grads[d], (((0,), (0,)), ((), ())), preferred_element_type=jnp.float32
        )

    mine_load.wait()
    for k in range(n_cuts):
        cut = slice(k * tile, (k + 1) * tile)
        total[cut, :] = times(mine[:, cut], 0)
    for k in range(n_cuts):
        for j in range(len(targets)):
            if k + window[j] < n_cuts:
                sends[j, k].wait_send()
                sends[j, k + window[j]].start()
    for d in offsets:
        for e in range(1, tensors):
            forwards[d, e].wait_recv()
    for k in range(n_cuts - 1):
        cut = slice(k * tile, (k + 1) * tile)
        for d in reversed(offsets):
            n_copies[d, k].wait_recv()
            if d == offsets[0]:
                total[cut, :] = (total[cut, :] + times(arrived[d - 1, k], d)) * factor
            else:
                total[cut, :] += times(arrived[d - 1, k], d)

    @pl.when(pipe < sections - 1)
    def _():
        for c in range(x_cuts):
            x_copy(c).wait_recv()
            wide = slice(c * step, (c + 1) * step)
            passed[:, wide] = (passed[:, wide].astype(jnp.float32) * factor).astype(passed.dtype)

    @pl.when(pipe == sections - 1)
    def _():
        passed[...] = jnp.zeros(passed.shape, passed.dtype)

    @pl.when(pipe > 0)
    def _():
        for c in range(x_cuts):
            x_copy(c).wait_send()

    for d in reversed(offsets):
        n_copies[d, n_cuts - 1].wait_recv()
    for j in range(len(targets)):
        for k in range(n_cuts - window[j], n_cuts):
            sends[j, k].wait_send()
    for d in offsets:
        g_copies[d].wait_send()
        for e in range(1, tensors):
            forwards[d, e].wait_send()


def finish(cuts, total, passed, grads, last, scale, grad_out, passed_out, closing, g_sem, p_sem):
    high = closing.shape[0]
    wide = passed.shape[1] // cuts
    ready = total.shape[0] - high
    copies = []
    for c in range(cuts):
        cut = pl.ds(c * wide, wide)
        copies.append(pltpu.make_async_copy(passed.at[:, cut], passed_out.at[0, :, cut], p_sem.at[c]))
    for c in range(ready // high):
        tall = pl.ds(c * high, high)
        copies.append(pltpu.make_async_copy(total.at[tall], grad_out.at[0, 0, tall], g_sem.at[c]))
    for copy in copies:
        copy.start()
    rest = total[ready:, :]
    for d in range(1, grads.shape[0]):
        rest = rest + lax.dot_general(
            last[d - 1], grads[d], (((0,), (0,)), ((), ())), preferred_element_type=jnp.float32
        )
    closing[...] = rest * scale[0:1, 0:1]
    copies.append(
        pltpu.make_async_copy(closing, grad_out.at[0, 0, pl.ds(ready, high)], g_sem.at[ready // high])
    )
    copies[-1].start()
    for copy in copies:
        copy.wait()


def in_kernels(replicas, tensors, sections, normed, w_value, grad_value, assistant_mask):
    _, rows, width = normed.shape
    heads = w_value.shape[2]
    owned = width // replicas
    x_cuts = pieces_of(width, LANES, 8)
    n_cuts = pieces_of(owned, LANES, 4)
    kind = normed.dtype
    vmem = pl.BlockSpec(memory_space=pltpu.VMEM)
    anywhere = pl.BlockSpec(memory_space=pl.ANY)
    dma = pltpu.SemaphoreType.DMA
    size = kind.itemsize
    held = size * (rows * owned * replicas + replicas * rows * heads + width * heads + rows * width)
    held += 4 * assistant_mask.size
    arguments = [
        pltpu.with_memory_space_constraint(array, pltpu.HBM)
        for array in (normed, w_value, grad_value, assistant_mask)
    ]
    results = pl.pallas_call(
        functools.partial(exchange, replicas, tensors, sections, x_cuts, n_cuts),
        out_shape=(
            pltpu.VMEM((owned, heads), jnp.float32),
            pltpu.VMEM((rows, width), kind),
            pltpu.VMEM((replicas, rows, heads), kind),
            pltpu.VMEM((replicas - 1, rows, owned // n_cuts), kind),
            pltpu.VMEM((8, LANES), jnp.float32),
        ),
        in_specs=[anywhere] * 4,
        out_specs=(vmem,) * 5,
        scratch_shapes=[
            pltpu.VMEM((rows, owned), kind),
            pltpu.VMEM((replicas - 1, max(n_cuts - 1, 1), rows, owned // n_cuts), kind),
            pltpu.VMEM((width, heads), kind),
            pltpu.VMEM((rows, width), kind),
            pltpu.VMEM((replicas, 8, LANES), jnp.int32),
            pltpu.VMEM(assistant_mask.shape[1:], jnp.int32),
            dma((3,)),
            dma((x_cuts,)),
            dma((replicas, n_cuts)),
            dma((replicas, n_cuts)),
            dma((replicas,)),
            dma((replicas,)),
            dma((replicas, tensors)),
            dma((replicas, tensors)),
            dma((replicas,)),
            dma((replicas,)),
            dma((x_cuts,)),
            dma((x_cuts,)),
        ],
        compiler_params=pltpu.CompilerParams(
            collective_id=0, has_side_effects=True, vmem_limit_bytes=held + (8 << 20)
        ),
        name="exchange",
    )(*arguments)
    out_cuts = pieces_of(width, LANES, 4)
    return pl.pallas_call(
        functools.partial(finish, out_cuts),
        out_shape=(
            jax.ShapeDtypeStruct((1, 1, owned, heads), jnp.float32),
            jax.ShapeDtypeStruct((1, rows, width), kind),
        ),
        in_specs=[vmem] * 5,
        out_specs=(anywhere, anywhere),
        scratch_shapes=[
            pltpu.VMEM((owned // n_cuts, heads), jnp.float32),
            dma((n_cuts,)),
            dma((out_cuts,)),
        ],
        compiler_params=pltpu.CompilerParams(vmem_limit_bytes=4 * owned * heads + (8 << 20)),
        name="finish",
    )(*results)


def with_collectives(normed, w_value, grad_value, assistant_mask):
    local_count = jnp.sum(assistant_mask, dtype=jnp.int32)
    mask_total = lax.psum(local_count, "dp")
    divisor = mask_total.astype(jnp.float32)
    inputs = normed[0]
    weight = w_value[0]
    upstream = grad_value[0]
    local_width = inputs.shape[1]
    replicas = lax.axis_size("dp")
    padded_rows = (local_width + replicas - 1) // replicas * replicas
    padded = jnp.pad(inputs, ((0, 0), (0, padded_rows - local_width)))
    weight_sum = lax.psum_scatter(
        lax.dot_general(
            padded, upstream, (((0,), (0,)), ((), ())), preferred_element_type=jnp.float32
        ).astype(jnp.bfloat16),
        "dp",
        scatter_dimension=0,
        tiled=True,
    ).astype(jnp.float32)
    total = jnp.zeros((upstream.shape[0], local_width), jnp.float32)
    for head in range(KV_HEADS):
        piece_up = upstream[:, head * HEAD : (head + 1) * HEAD]
        piece_w = weight[:, head * HEAD : (head + 1) * HEAD]
        part = lax.dot_general(
            piece_up, piece_w, (((1,), (1,)), ((), ())), preferred_element_type=jnp.float32
        ).astype(jnp.bfloat16)
        total = total + part.astype(jnp.float32)
    weight_grad = weight_sum / divisor
    input_grad = (total / divisor).astype(jnp.bfloat16)
    passed = from_behind(input_grad, "pipe", -1)
    return (weight_grad[None, None], passed[None])


def solution(mesh):
    replicas, tensors, sections = mesh.shape["dp"], mesh.shape["tensor"], mesh.shape["pipe"]

    def local(normed, w_value, grad_value, assistant_mask):
        _, rows, width = normed.shape
        aligned = width % (replicas * LANES) == 0 and rows % (tensors * PACK) == 0
        aligned = aligned and replicas & (replicas - 1) == 0
        if aligned and min(replicas, tensors, sections) > 1:
            return in_kernels(replicas, tensors, sections, normed, w_value, grad_value, assistant_mask)
        return with_collectives(normed, w_value, grad_value, assistant_mask)

    return jax.shard_map(
        local,
        mesh=mesh,
        in_specs=(
            P("pipe", "dp", "tensor"),
            P("pipe", "tensor", None),
            P("pipe", "dp", None),
            P("dp", None, None),
        ),
        out_specs=(P("pipe", "tensor", "dp", None), P("pipe", "dp", "tensor")),
        check_vma=False,
    )
```
